32 devices in a mesh: section: 8 (over z, x), expert: 4 (over y, core).
Axes of the slice: x: 2, y: 2, z: 4, core: 2. Of those that a mesh axis runs over, the one named last changes fastest.
Arguments:
- tokens: bfloat16 [128, 6144], P('section', 'expert'), may hold values from -6 to 6
- gains: float32 [6144], replicated, may hold values from 0.1 to 1.9
- w_gate: bfloat16 [4, 6144, 2048], P('expert', None, 'section'), may hold values from -0.078125 to 0.078125
- w_up: bfloat16 [4, 6144, 2048], P('expert', None, 'section'), may hold values from -0.078125 to 0.078125
- w_down: bfloat16 [4, 2048, 6144], P('expert', 'section'), may hold values from -0.125 to 0.125
- expert_ids: int32 [128, 2], replicated, may hold values from 0 to 3, all different within a row; in each aligned block of 16 rows (0 to 15, 16 to 31, ...) at most 12 rows name the same one
- gate_ints: int32 [128, 2], replicated, may hold values from 1 to 65535
Outputs:
- mixed: bfloat16 [128, 6144], P('section', 'expert')
The draws below stay inside these ranges and needn't reach their ends.
Inputs may be any that keep to these rules, and one draw needn't show every extreme that they name: `expert_ids`: in each aligned block of 16 token rows (the rows of one index of section), no expert is named by more than 12 rows.
All inputs are finite; a program needn't handle non-finite values.
Results may differ from the reference program's by a relative error of at most 0.0042.
Values may be sent and summed in bfloat16 or wider, within the bound.
A program may use at most 128 MiB of HBM per device.

```python
import math
import jax
import jax.numpy as jnp
import numpy as np
from jax import lax

D = 6144
TOP = 2
TOK_DEV = 16
CAP = 12
HID = 2048
EXPERTS = 4
TOKENS = 128


def set_ends(array, own_key, smallest, top_value):
    dims = array.shape
    index_at = [jax.random.randint(jax.random.fold_in(own_key, axis), (), 0, dims[axis]) for axis in range(len(dims))]
    array = array.at[tuple(index_at)].set(smallest)
    longest = dims.index(max(dims))
    index_at[longest] = (index_at[longest] + 1) % dims[longest]
    return array.at[tuple(index_at)].set(top_value)


def steps_of(stream_key, extent, split, low, high):
    loudness = 1.0
    for dim, parts in split:
        heights = jax.random.uniform(jax.random.fold_in(jax.random.fold_in(stream_key, 6), dim), (parts,), jnp.float32, low / len(split), high / len(split))
        loudness = loudness * jnp.repeat(jnp.exp(heights), extent[dim] // parts).reshape((-1,) + (1,) * (len(extent) - 1 - dim))
    return loudness


def assign_block(own_key, own, number, rows, count, top, bound, lean):
    order = jax.random.permutation(own_key, count)
    heavy_load, usual = load_shares(count, rows * top, bound, lean, True), load_shares(count, rows * top, bound, lean, False)
    places = jnp.arange(count)

    def named(tallies, offset_by):
        used = int((tallies > 0).sum())
        fixed = max(1, used // 4)
        moved = fixed + (places - fixed + offset_by * (used - fixed)) % max(1, count - fixed)
        return jnp.zeros((count,), jnp.int32).at[order[jnp.where(places < fixed, places, moved)]].set(jnp.asarray(tallies, jnp.int32))

    tallies = jnp.where(number % 4 == 0, named(heavy_load, number // 4), named(usual, number - number // 4 - 1))
    mixed = jax.random.permutation(jax.random.fold_in(own, 3), count)
    giver, sink = mixed[0:count // 2 * 2:2], mixed[1:count // 2 * 2:2]
    slack = jnp.minimum(tallies[giver] - 1, bound - tallies[sink]) // 2
    slack = jnp.where((giver == order[0]) | (sink == order[0]) | (tallies[sink] == 0), 0, jnp.maximum(slack, 0))
    moved = jax.random.randint(jax.random.fold_in(own, 4), (count // 2,), 0, 1 << 20) % (slack + 1)
    tallies = tallies.at[giver].add(-moved).at[sink].add(moved)
    labels = jnp.searchsorted(jnp.cumsum(tallies), jnp.arange(rows * top), side="right").astype(jnp.int32)
    listing = labels.reshape(top, rows).T
    listing = listing[jax.random.permutation(jax.random.fold_in(own, 1), rows)]
    offset_by = jax.random.randint(jax.random.fold_in(own, 2), (rows, 1), 0, top)
    return jnp.take_along_axis(listing, (jnp.arange(top)[None, :] + offset_by) % top, axis=1)


def load_shares(count, total, most, slope, full):
    portions = [(1 << 20) // math.isqrt(standing ** slope) + 1 for standing in range(1, count + 1)]
    largest = most if full else min(most, max(-(-total // count), total * portions[0] // sum(portions)))
    least = 1 if total - largest >= count - 1 else 0
    holding, surplus = [largest] + [least] * (count - 1), total - largest - least * (count - 1)
    while surplus > 0:
        movable = [i for i in range(1, count) if holding[i] < largest] or [i for i in range(1, count) if holding[i] < most]
        pool, left = sum([portions[i] for i in movable]), surplus
        for i in movable:
            extra = min(most - holding[i], max(1, left * portions[i] // pool), surplus)
            holding[i] = holding[i] + extra
            surplus = surplus - extra
    return np.array(holding)


def noise(rng, shape, scale, most, shards=(), kind=jnp.bfloat16):
    drawn = scale * jax.random.normal(rng, shape, jnp.float32)
    if shards:
        drawn = drawn * steps_of(rng, shape, shards, -0.22, 0.18)
    return jnp.clip(drawn, -most, most).astype(kind)


def setup_inputs(seed: int = 0) -> dict:
    splits = jax.random.split(jax.random.key(seed), 8)
    tokens = noise(splits[0], (TOKENS, D), 1.0, 6.0, ((0, 8), (1, 4)))
    gains = jnp.clip(1.0 + 0.18 * jax.random.normal(splits[1], (D,), jnp.float32), 0.1, 1.9)
    w_gate = noise(splits[2], (EXPERTS, D, HID), D ** -0.5, 0.078125, ((0, 4), (2, 8)))
    w_up = noise(splits[3], (EXPERTS, D, HID), D ** -0.5, 0.078125, ((0, 4), (2, 8)))
    w_down = noise(splits[4], (EXPERTS, HID, D), HID ** -0.5, 0.125, ((0, 4), (1, 8)))
    expert_ids_keys = jax.random.split(jax.random.fold_in(splits[5], 1), TOKENS // TOK_DEV)
    expert_ids_turns = jax.random.permutation(jax.random.fold_in(splits[5], 3), TOKENS // TOK_DEV)
    expert_ids = jax.vmap(lambda own, number: assign_block(jax.random.fold_in(splits[5], 2), own, number, TOK_DEV, EXPERTS, TOP, CAP, 2))(expert_ids_keys, expert_ids_turns).reshape((TOKENS, TOP))
    gate_ints = set_ends(jax.random.randint(splits[6], (TOKENS, TOP), 1, 65536), jax.random.fold_in(splits[6], 1), 1, 65535).astype(jnp.int32)
    return dict(tokens=tokens, gains=gains, w_gate=w_gate, w_up=w_up, w_down=w_down, expert_ids=expert_ids, gate_ints=gate_ints)


def reference(tokens, gains, w_gate, w_up, w_down, expert_ids, gate_ints):
    floated = tokens.astype(jnp.float32)
    mean_sq = lax.optimization_barrier(jnp.mean(floated * floated, axis=-1, keepdims=True))
    normed = (floated * lax.rsqrt(mean_sq + 1e-05) * gains).astype(jnp.bfloat16)
    scaled = gate_ints.astype(jnp.float32) / 65536.0

    def one_expert(running, expert_no):
        gate_val = jnp.dot(normed, w_gate[expert_no], preferred_element_type=jnp.float32)
        up_val = jnp.dot(normed, w_up[expert_no], preferred_element_type=jnp.float32)
        hidden_act = (jax.nn.silu(gate_val) * up_val).astype(jnp.bfloat16)
        result = jnp.dot(hidden_act, w_down[expert_no], preferred_element_type=jnp.float32)
        weight = lax.optimization_barrier(jnp.sum(jnp.where(expert_ids == expert_no, scaled, 0.0), axis=-1))
        return (running + result * weight[:, None], None)
    initial = jnp.zeros(floated.shape, jnp.float32)
    running, _ = lax.scan(one_expert, initial, jnp.arange(EXPERTS, dtype=jnp.int32))
    return (floated + running).astype(jnp.bfloat16)
```

```python
import functools

import jax
import jax.numpy as jnp
from jax import lax
from jax.experimental import pallas as pl
from jax.experimental.pallas import tpu as pltpu
from jax.sharding import PartitionSpec as P

EPS = 1e-05
MESH = pl.DeviceIdType.MESH
BF16 = jnp.bfloat16
F32 = jnp.float32
TILE = 128


def flip(index, mask):
    bit = 1
    while bit <= mask:
        if mask & bit:
            index = index + bit - 2 * bit * lax.rem(lax.div(index, bit), 2)
        bit *= 2
    return index


def kernel(
    depth, tok, gains, wg, wu, wd, ids, ints, out,
    x, xn, w_in, w_out, gains_v, ids_v, ints_v, inner, weight,
    own, sib_s, sib_r, b_s, b_r, a_s, a_r, z_s, z_r,
    load_sem, in_recv, in_sib_recv, in_z_send, in_a_send, in_b_send, in_sib_send,
    sib_send, sib_recv, b_send, b_recv, a_send, a_recv, z_send, z_recv,
):
    section, expert = lax.axis_index("section"), lax.axis_index("expert")
    z, px = lax.div(section, 2), lax.rem(section, 2)
    py, core = lax.div(expert, 2), lax.rem(expert, 2)
    rows, width = tok.shape
    total = x.shape[1]
    hid = wg.shape[2]
    features = x.shape[0] * width
    i = py * (1 - core) + px * core
    j = px * (1 - core) + py * core

    def place(zz, ii, jj):
        yy = ii * (1 - core) + jj * core
        xx = jj * (1 - core) + ii * core
        return zz * 2 + xx, yy

    def rows_of(sec):
        return pl.ds(pl.multiple_of(sec * rows, rows), rows)

    def device(zz, ii, jj):
        sec, yy = place(zz, ii, jj)
        return sec, yy * 2 + core

    a_dev = device(z, i, 1 - j)
    b_dev = device(z, 1 - i, j)
    sib_dev = (section, py * 2 + 1 - core)
    z_devs = [(flip(z, k) * 2 + px, expert) for k in range(1, depth)]

    loads = [
        pltpu.make_async_copy(tok, x.at[expert, rows_of(section)], load_sem.at[0]),
        pltpu.make_async_copy(wg.at[0], w_in.at[:, pl.ds(0, hid)], load_sem.at[1]),
        pltpu.make_async_copy(wu.at[0], w_in.at[:, pl.ds(hid, hid)], load_sem.at[2]),
        pltpu.make_async_copy(gains, gains_v, load_sem.at[3]),
        pltpu.make_async_copy(ids, ids_v, load_sem.at[4]),
        pltpu.make_async_copy(ints, ints_v, load_sem.at[5]),
    ] + [
        pltpu.make_async_copy(
            wd.at[0, :, pl.ds(e * width, width)], w_out.at[e], load_sem.at[6 + e]
        )
        for e in range(x.shape[0])
    ]
    for load in loads:
        load.start()

    barrier = pltpu.get_barrier_semaphore()
    partners = z_devs + [a_dev, b_dev, sib_dev]
    for partner in partners:
        pl.semaphore_signal(barrier, inc=1, device_id=partner, device_id_type=MESH)
    pl.semaphore_wait(barrier, len(partners))

    pending = []

    def block(zz, ii, jj):
        sec, yy = place(zz, ii, jj)
        return x.at[yy * 2 + core, rows_of(sec)]

    def push(source, zz, ii, jj, send_sem, target):
        copy = pltpu.make_async_remote_copy(
            src_ref=source, dst_ref=block(zz, ii, jj), send_sem=send_sem,
            recv_sem=in_recv.at[(zz * 2 + ii) * 2 + jj],
            device_id=target, device_id_type=MESH,
        )
        copy.start()
        pending.append(copy)

    def push_sib(source, zz, ii, jj):
        sec, yy = place(zz, ii, jj)
        copy = pltpu.make_async_remote_copy(
            src_ref=source, dst_ref=block(zz, ii, jj), send_sem=in_sib_send.at[sec * 2 + yy],
            recv_sem=in_sib_recv.at[sec * 2 + yy],
            device_id=sib_dev, device_id_type=MESH,
        )
        copy.start()
        pending.append(copy)

    def arrived(zz, ii, jj):
        here = block(zz, ii, jj)
        pltpu.make_async_remote_copy(
            src_ref=here, dst_ref=here, send_sem=in_z_send.at[0],
            recv_sem=in_recv.at[(zz * 2 + ii) * 2 + jj],
            device_id=sib_dev, device_id_type=MESH,
        ).wait_recv()
        return here

    for k in range(1, depth):
        push(tok, z, i, j, in_z_send.at[k - 1], z_devs[k - 1])
    push(tok, z, i, j, in_a_send.at[0], a_dev)
    push(tok, z, i, j, in_b_send.at[0], b_dev)
    push_sib(tok, z, i, j)
    for k in range(1, depth):
        zz = flip(z, k)
        here = arrived(zz, i, j)
        push(here, zz, i, j, in_a_send.at[k], a_dev)
        push(here, zz, i, j, in_b_send.at[k], b_dev)
        push_sib(here, zz, i, j)
    for k in range(depth):
        zz = flip(z, k)
        here = arrived(zz, i, 1 - j)
        push(here, zz, i, 1 - j, in_b_send.at[depth + k], b_dev)
        push_sib(here, zz, i, 1 - j)
    for jj in (j, 1 - j):
        for k in range(depth):
            zz = flip(z, k)
            push_sib(arrived(zz, 1 - i, jj), zz, 1 - i, jj)

    for load in loads:
        load.wait()
    chosen = jnp.where(ids_v[...] == expert, ints_v[...].astype(F32) / 65536.0, 0.0)
    row = jnp.sum(chosen, axis=0, keepdims=True)
    weight[...] = jnp.broadcast_to(row, (8, total)).T[:, :1]

    for sec in range(2 * depth):
        for yy in range(2):
            here = x.at[yy * 2 + 1 - core, rows_of(sec)]
            pltpu.make_async_remote_copy(
                src_ref=here, dst_ref=here, send_sem=in_z_send.at[0],
                recv_sem=in_sib_recv.at[sec * 2 + yy],
                device_id=sib_dev, device_id_type=MESH,
            ).wait_recv()

    slices = range(x.shape[0])

    def tiles(body):
        if total == TILE:
            body(pl.ds(0, TILE))
        else:
            @pl.loop(0, total // TILE)
            def _(t):
                body(pl.ds(pl.multiple_of(t * TILE, TILE), TILE))

    def hidden(span):
        squares = 0.0
        for e in slices:
            part = x[e, span].astype(F32)
            squares = squares + jnp.sum(part * part, axis=-1, keepdims=True)
        scale = lax.rsqrt(squares / features + EPS)
        both = jnp.zeros((TILE, 2 * hid), F32)
        for e in slices:
            cols = pl.ds(e * width, width)
            xn[e] = (x[e, span].astype(F32) * scale * gains_v[:, cols]).astype(BF16)
            both = both + jnp.dot(xn[e], w_in[cols], preferred_element_type=F32)
        gate, up = both[:, :hid], both[:, hid:]
        inner[span] = (gate / (1.0 + jnp.exp(-gate)) * up).astype(BF16)

    tiles(hidden)

    def down(e, target, kind):
        def one(span):
            target[span] = (
                jnp.dot(inner[span], w_out[e], preferred_element_type=F32) * weight[span]
            ).astype(kind)
        tiles(one)

    for n, yy in enumerate((1 - py, py)):
        down(yy * 2 + 1 - core, sib_s.at[yy], BF16)
        copy = pltpu.make_async_remote_copy(
            src_ref=sib_s.at[yy], dst_ref=sib_r.at[yy], send_sem=sib_send.at[yy],
            recv_sem=sib_recv.at[yy], device_id=sib_dev, device_id_type=MESH,
        )
        copy.start()
        pending.append(copy)
    for yy in (1 - py, py):
        down(yy * 2 + core, own.at[yy], F32)
    for yy in (1 - py, py):
        pltpu.make_async_remote_copy(
            src_ref=sib_s.at[yy], dst_ref=sib_r.at[yy], send_sem=sib_send.at[yy],
            recv_sem=sib_recv.at[yy], device_id=sib_dev, device_id_type=MESH,
        ).wait_recv()

    def pair(zz, ii, jj):
        sec, yy = place(zz, ii, jj)
        span = rows_of(sec)
        return own[yy, span] + sib_r[yy, span].astype(F32)

    def send(value, source, source_slot, target, target_slot, send_sem, recv_sem, dev):
        source[source_slot] = value.astype(BF16)
        copy = pltpu.make_async_remote_copy(
            src_ref=source.at[source_slot], dst_ref=target.at[target_slot],
            send_sem=send_sem.at[source_slot], recv_sem=recv_sem.at[target_slot],
            device_id=dev, device_id_type=MESH,
        )
        copy.start()
        pending.append(copy)

    def take(target, slot, recv_sem):
        pltpu.make_async_remote_copy(
            src_ref=target.at[slot], dst_ref=target.at[slot], send_sem=in_z_send.at[0],
            recv_sem=recv_sem.at[slot], device_id=sib_dev, device_id_type=MESH,
        ).wait_recv()
        return target[slot].astype(F32)

    order = list(range(1, depth)) + [0]
    for jj in (1 - j, j):
        for k in order:
            zz = flip(z, k)
            slot = jj * depth + zz
            send(pair(zz, 1 - i, jj), b_s, slot, b_r, slot, b_send, b_recv, b_dev)
    for k in order:
        zz = flip(z, k)
        value = pair(zz, i, 1 - j) + take(b_r, (1 - j) * depth + zz, b_recv)
        send(value, a_s, zz, a_r, zz, a_send, a_recv, a_dev)
    for k in order:
        zz = flip(z, k)
        value = pair(zz, i, j) + take(b_r, j * depth + zz, b_recv) + take(a_r, zz, a_recv)
        if k:
            send(value, z_s, zz, z_r, z, z_send, z_recv, z_devs[k - 1])
    for k in range(1, depth):
        value = value + take(z_r, flip(z, k), z_recv)
    out[...] = (x[expert, rows_of(section)].astype(F32) + value).astype(BF16)
    for copy in pending:
        copy.wait_send()


def body(tokens, gains, w_gate, w_up, w_down, expert_ids, gate_ints, *, sections, experts):
    rows, width = tokens.shape
    hid = w_gate.shape[2]
    features = gains.shape[0]
    total = expert_ids.shape[0]
    top = expert_ids.shape[1]
    depth = sections // 2
    dma = pltpu.SemaphoreType.DMA
    blocks = 4 * depth
    return pl.pallas_call(
        functools.partial(kernel, depth),
        out_shape=jax.ShapeDtypeStruct((rows, width), BF16),
        in_specs=[pl.BlockSpec(memory_space=pl.ANY)] * 7,
        out_specs=pl.BlockSpec(memory_space=pltpu.VMEM),
        scratch_shapes=[
            pltpu.VMEM((experts, total, width), BF16),
            pltpu.VMEM((experts, TILE, width), BF16),
            pltpu.VMEM((features, 2 * hid), BF16),
            pltpu.VMEM((experts, hid, width), BF16),
            pltpu.VMEM((1, features), F32),
            pltpu.VMEM((top, total), jnp.int32),
            pltpu.VMEM((top, total), jnp.int32),
            pltpu.VMEM((total, hid), BF16),
            pltpu.VMEM((total, 1), F32),
            pltpu.VMEM((2, total, width), F32),
            pltpu.VMEM((2, total, width), BF16),
            pltpu.VMEM((2, total, width), BF16),
            pltpu.VMEM((2 * depth, rows, width), BF16),
            pltpu.VMEM((2 * depth, rows, width), BF16),
            pltpu.VMEM((depth, rows, width), BF16),
            pltpu.VMEM((depth, rows, width), BF16),
            pltpu.VMEM((depth, rows, width), BF16),
            pltpu.VMEM((depth, rows, width), BF16),
            dma((6 + experts,)),
            dma((blocks,)), dma((blocks,)),
            dma((depth,)), dma((depth,)), dma((2 * depth,)), dma((blocks,)),
            dma((2,)), dma((2,)),
            dma((2 * depth,)), dma((2 * depth,)),
            dma((depth,)), dma((depth,)),
            dma((depth,)), dma((depth,)),
        ],
        compiler_params=pltpu.CompilerParams(
            collective_id=0, has_side_effects=True, vmem_limit_bytes=62 * 1024 * 1024,
        ),
    )(tokens, gains.reshape(1, features), w_gate, w_up, w_down, expert_ids.T, gate_ints.T)


def solution(mesh):
    in_specs = (
        P("section", "expert"),
        P(),
        P("expert", None, "section"),
        P("expert", None, "section"),
        P("expert", "section", None),
        P(),
        P(),
    )
    run = functools.partial(
        body, sections=mesh.shape["section"], experts=mesh.shape["expert"]
    )
    return jax.shard_map(
        run, mesh=mesh, in_specs=in_specs, out_specs=P("section", "expert"), check_vma=False
    )
```

```python
import functools

import jax
import jax.numpy as jnp
from jax import lax
from jax.experimental import pallas as pl
from jax.experimental.pallas import tpu as pltpu
from jax.sharding import PartitionSpec as P

EPS = 1e-05
MESH = pl.DeviceIdType.MESH
BF16 = jnp.bfloat16
F32 = jnp.float32
TILE = 128
LANES = 128


def flip(index, mask):
    bit = 1
    while bit <= mask:
        if mask & bit:
            index = index + bit - 2 * bit * lax.rem(lax.div(index, bit), 2)
        bit *= 2
    return index


def kernel(
    depth, tok, gains, wg, wu, wd, ids, ints, out,
    x, xn, w_in, w_out, gains_v, ids_v, ints_v, inner, weight, ss, acc,
    own, sib_s, sib_r, b_s, b_r, a_s, a_r, z_s, z_r,
    load_sem, in_recv, in_sib_recv, in_z_send, in_a_send, in_b_send, in_sib_send,
    sib_send, sib_recv, b_send, b_recv, a_send, a_recv, z_send, z_recv,
):
    section, expert = lax.axis_index("section"), lax.axis_index("expert")
    z, px = lax.div(section, 2), lax.rem(section, 2)
    py, core = lax.div(expert, 2), lax.rem(expert, 2)
    rows, width = tok.shape
    total = x.shape[1]
    hid = wg.shape[2]
    features = x.shape[0] * width
    i = py * (1 - core) + px * core
    j = px * (1 - core) + py * core

    def place(zz, ii, jj):
        yy = ii * (1 - core) + jj * core
        xx = jj * (1 - core) + ii * core
        return zz * 2 + xx, yy

    def rows_of(sec):
        return pl.ds(pl.multiple_of(sec * rows, rows), rows)

    def device(zz, ii, jj):
        sec, yy = place(zz, ii, jj)
        return sec, yy * 2 + core

    a_dev = device(z, i, 1 - j)
    b_dev = device(z, 1 - i, j)
    sib_dev = (section, py * 2 + 1 - core)
    z_devs = [(flip(z, k) * 2 + px, expert) for k in range(1, depth)]

    own_block = x.at[expert, rows_of(section)]
    tok_load = pltpu.make_async_copy(tok, own_block, load_sem.at[0])
    tok_load.start()
    loads = [
        pltpu.make_async_copy(gains, gains_v, load_sem.at[3]),
        pltpu.make_async_copy(ids, ids_v, load_sem.at[4]),
        pltpu.make_async_copy(ints, ints_v, load_sem.at[5]),
        pltpu.make_async_copy(wg.at[0], w_in.at[:, pl.ds(0, hid)], load_sem.at[1]),
        pltpu.make_async_copy(wu.at[0], w_in.at[:, pl.ds(hid, hid)], load_sem.at[2]),
    ] + [
        pltpu.make_async_copy(
            wd.at[0, :, pl.ds(e * width, width)], w_out.at[e], load_sem.at[6 + e]
        )
        for e in range(x.shape[0])
    ]

    barrier = pltpu.get_barrier_semaphore()
    partners = z_devs + [a_dev, b_dev, sib_dev]
    for partner in partners:
        pl.semaphore_signal(barrier, inc=1, device_id=partner, device_id_type=MESH)
    pl.semaphore_wait(barrier, len(partners))
    tok_load.wait()

    pending = []

    def block(zz, ii, jj):
        sec, yy = place(zz, ii, jj)
        return x.at[yy * 2 + core, rows_of(sec)]

    def push(source, zz, ii, jj, send_sem, target):
        copy = pltpu.make_async_remote_copy(
            src_ref=source, dst_ref=block(zz, ii, jj), send_sem=send_sem,
            recv_sem=in_recv.at[(zz * 2 + ii) * 2 + jj],
            device_id=target, device_id_type=MESH,
        )
        copy.start()
        pending.append(copy)

    def push_sib(source, zz, ii, jj):
        sec, yy = place(zz, ii, jj)
        copy = pltpu.make_async_remote_copy(
            src_ref=source, dst_ref=block(zz, ii, jj), send_sem=in_sib_send.at[sec * 2 + yy],
            recv_sem=in_sib_recv.at[sec * 2 + yy],
            device_id=sib_dev, device_id_type=MESH,
        )
        copy.start()
        pending.append(copy)

    def arrived(zz, ii, jj):
        here = block(zz, ii, jj)
        pltpu.make_async_remote_copy(
            src_ref=here, dst_ref=here, send_sem=in_z_send.at[0],
            recv_sem=in_recv.at[(zz * 2 + ii) * 2 + jj],
            device_id=sib_dev, device_id_type=MESH,
        ).wait_recv()
        return here

    for k in range(1, depth):
        push(own_block, z, i, j, in_z_send.at[k - 1], z_devs[k - 1])
    push(own_block, z, i, j, in_a_send.at[0], a_dev)
    push(own_block, z, i, j, in_b_send.at[0], b_dev)
    push_sib(own_block, z, i, j)
    for load in loads:
        load.start()
    for k in range(1, depth):
        zz = flip(z, k)
        here = arrived(zz, i, j)
        push(here, zz, i, j, in_a_send.at[k], a_dev)
        push(here, zz, i, j, in_b_send.at[k], b_dev)
        push_sib(here, zz, i, j)
    for k in range(depth):
        zz = flip(z, k)
        here = arrived(zz, i, 1 - j)
        push(here, zz, i, 1 - j, in_b_send.at[depth + k], b_dev)
        push_sib(here, zz, i, 1 - j)

    def tiles(body):
        if total == TILE:
            body(pl.ds(0, TILE))
        else:
            @pl.loop(0, total // TILE)
            def _(t):
                body(pl.ds(pl.multiple_of(t * TILE, TILE), TILE))

    def project(e, first):
        def one(span):
            squares = jnp.zeros((TILE, LANES), F32) if first else ss[span]
            for c in range(0, width, LANES):
                cols = pl.ds(c, LANES)
                part = x[e, span, cols].astype(F32)
                squares = squares + part * part
                xn[:, cols] = (part * gains_v[e, :, cols]).astype(BF16)
            ss[span] = squares
            product = jnp.dot(
                xn[...], w_in[pl.ds(pl.multiple_of(e * width, width), width)],
                preferred_element_type=F32,
            )
            acc[span] = product if first else acc[span] + product
        tiles(one)

    def forward(jj, ks):
        for k in ks:
            zz = flip(z, k)
            push_sib(arrived(zz, 1 - i, jj), zz, 1 - i, jj)

    def sib_slice(yy):
        for sec in range(2 * depth):
            here = x.at[yy * 2 + 1 - core, rows_of(sec)]
            pltpu.make_async_remote_copy(
                src_ref=here, dst_ref=here, send_sem=in_z_send.at[0],
                recv_sem=in_sib_recv.at[sec * 2 + yy],
                device_id=sib_dev, device_id_type=MESH,
            ).wait_recv()

    for load in loads:
        load.wait()
    chosen = jnp.where(ids_v[...] == expert, ints_v[...].astype(F32) / 65536.0, 0.0)
    row = jnp.sum(chosen, axis=0, keepdims=True)
    weight[...] = jnp.broadcast_to(row, (8, total)).T[:, :1]

    forward(j, range(depth))
    project(py * 2 + core, True)
    forward(1 - j, range(depth // 2))
    sib_slice(py)
    project(py * 2 + 1 - core, False)
    forward(1 - j, range(depth // 2, depth))
    project((1 - py) * 2 + core, False)
    sib_slice(1 - py)
    project((1 - py) * 2 + 1 - core, False)

    def activate(span):
        mean_sq = jnp.sum(ss[span], axis=-1, keepdims=True) / features
        both = acc[span] * lax.rsqrt(mean_sq + EPS)
        gate, up = both[:, :hid], both[:, hid:]
        inner[span] = (gate / (1.0 + jnp.exp(-gate)) * up).astype(BF16)

    tiles(activate)

    def down(e, target, kind):
        def one(span):
            target[span] = (
                jnp.dot(inner[span], w_out[e], preferred_element_type=F32) * weight[span]
            ).astype(kind)
        tiles(one)

    def sib_copy(yy):
        return pltpu.make_async_remote_copy(
            src_ref=sib_s.at[yy], dst_ref=sib_r.at[yy], send_sem=sib_send.at[yy],
            recv_sem=sib_recv.at[yy], device_id=sib_dev, device_id_type=MESH,
        )

    def partials(yy):
        down(yy * 2 + 1 - core, sib_s.at[yy], BF16)
        copy = sib_copy(yy)
        copy.start()
        pending.append(copy)
        down(yy * 2 + core, own.at[yy], F32)
        copy.wait_recv()

    def pair(zz, ii, jj):
        sec, yy = place(zz, ii, jj)
        span = rows_of(sec)
        return own[yy, span] + sib_r[yy, span].astype(F32)

    def send(value, source, source_slot, target, target_slot, send_sem, recv_sem, dev):
        source[source_slot] = value.astype(BF16)
        copy = pltpu.make_async_remote_copy(
            src_ref=source.at[source_slot], dst_ref=target.at[target_slot],
            send_sem=send_sem.at[source_slot], recv_sem=recv_sem.at[target_slot],
            device_id=dev, device_id_type=MESH,
        )
        copy.start()
        pending.append(copy)

    def take(target, slot, recv_sem):
        pltpu.make_async_remote_copy(
            src_ref=target.at[slot], dst_ref=target.at[slot], send_sem=in_z_send.at[0],
            recv_sem=recv_sem.at[slot], device_id=sib_dev, device_id_type=MESH,
        ).wait_recv()
        return target[slot].astype(F32)

    order = list(range(1, depth)) + [0]
    for yy, jj in ((1 - py, 1 - j), (py, j)):
        partials(yy)
        for k in order:
            zz = flip(z, k)
            slot = jj * depth + zz
            send(pair(zz, 1 - i, jj), b_s, slot, b_r, slot, b_send, b_recv, b_dev)
    for k in order:
        zz = flip(z, k)
        value = pair(zz, i, 1 - j) + take(b_r, (1 - j) * depth + zz, b_recv)
        send(value, a_s, zz, a_r, zz, a_send, a_recv, a_dev)
    for k in order:
        zz = flip(z, k)
        value = pair(zz, i, j) + take(b_r, j * depth + zz, b_recv) + take(a_r, zz, a_recv)
        if k:
            send(value, z_s, zz, z_r, z, z_send, z_recv, z_devs[k - 1])
    for k in range(1, depth):
        value = value + take(z_r, flip(z, k), z_recv)
    out[...] = (x[expert, rows_of(section)].astype(F32) + value).astype(BF16)
    for copy in pending:
        copy.wait_send()


def body(tokens, gains, w_gate, w_up, w_down, expert_ids, gate_ints, *, sections, experts):
    rows, width = tokens.shape
    hid = w_gate.shape[2]
    features = gains.shape[0]
    total = expert_ids.shape[0]
    top = expert_ids.shape[1]
    depth = sections // 2
    dma = pltpu.SemaphoreType.DMA
    blocks = 4 * depth
    return pl.pallas_call(
        functools.partial(kernel, depth),
        out_shape=jax.ShapeDtypeStruct((rows, width), BF16),
        in_specs=[pl.BlockSpec(memory_space=pl.ANY)] * 7,
        out_specs=pl.BlockSpec(memory_space=pltpu.VMEM),
        scratch_shapes=[
            pltpu.VMEM((experts, total, width), BF16),
            pltpu.VMEM((TILE, width), BF16),
            pltpu.VMEM((features, 2 * hid), BF16),
            pltpu.VMEM((experts, hid, width), BF16),
            pltpu.VMEM((experts, 1, width), F32),
            pltpu.VMEM((top, total), jnp.int32),
            pltpu.VMEM((top, total), jnp.int32),
            pltpu.VMEM((total, hid), BF16),
            pltpu.VMEM((total, 1), F32),
            pltpu.VMEM((total, LANES), F32),
            pltpu.VMEM((total, 2 * hid), F32),
            pltpu.VMEM((2, total, width), F32),
            pltpu.VMEM((2, total, width), BF16),
            pltpu.VMEM((2, total, width), BF16),
            pltpu.VMEM((2 * depth, rows, width), BF16),
            pltpu.VMEM((2 * depth, rows, width), BF16),
            pltpu.VMEM((depth, rows, width), BF16),
            pltpu.VMEM((depth, rows, width), BF16),
            pltpu.VMEM((depth, rows, width), BF16),
            pltpu.VMEM((depth, rows, width), BF16),
            dma((6 + experts,)),
            dma((blocks,)), dma((blocks,)),
            dma((depth,)), dma((depth,)), dma((2 * depth,)), dma((blocks,)),
            dma((2,)), dma((2,)),
            dma((2 * depth,)), dma((2 * depth,)),
            dma((depth,)), dma((depth,)),
            dma((depth,)), dma((depth,)),
        ],
        compiler_params=pltpu.CompilerParams(
            collective_id=0, has_side_effects=True, vmem_limit_bytes=62 * 1024 * 1024,
        ),
    )(tokens, gains.reshape(experts, 1, width), w_gate, w_up, w_down, expert_ids.T, gate_ints.T)


def solution(mesh):
    in_specs = (
        P("section", "expert"),
        P(),
        P("expert", None, "section"),
        P("expert", None, "section"),
        P("expert", "section", None),
        P(),
        P(),
    )
    run = functools.partial(
        body, sections=mesh.shape["section"], experts=mesh.shape["expert"]
    )
    return jax.shard_map(
        run, mesh=mesh, in_specs=in_specs, out_specs=P("section", "expert"), check_vma=False
    )
```

```python
import functools

import jax
import jax.numpy as jnp
from jax import lax
from jax.experimental import pallas as pl
from jax.experimental.pallas import tpu as pltpu
from jax.sharding import PartitionSpec as P

EPS = 1e-05
MESH = pl.DeviceIdType.MESH
BF16 = jnp.bfloat16
F32 = jnp.float32
TILE = 128
LANES = 128


def flip(index, mask):
    bit = 1
    while bit <= mask:
        if mask & bit:
            index = index + bit - 2 * bit * lax.rem(lax.div(index, bit), 2)
        bit *= 2
    return index


def kernel(
    depth, tok, gains, wg, wu, wd, ids, ints, out,
    x, xn, w_in, w_out, gains_v, ids_v, ints_v, inner, weight, ss, acc,
    own, b_s, b_r, a_s, a_r, z_s, z_r,
    load_sem, in_recv, in_sib_recv, in_z_send, in_a_send, in_b_send, in_sib_send,
    w_send, w_recv, inner_send, inner_recv, b_send, b_recv, a_send, a_recv, z_send, z_recv,
):
    section, expert = lax.axis_index("section"), lax.axis_index("expert")
    z, px = lax.div(section, 2), lax.rem(section, 2)
    py, core = lax.div(expert, 2), lax.rem(expert, 2)
    rows, width = tok.shape
    total = x.shape[1]
    hid = wg.shape[2]
    features = x.shape[0] * width
    i = py * (1 - core) + px * core
    j = px * (1 - core) + py * core

    def place(zz, ii, jj):
        yy = ii * (1 - core) + jj * core
        xx = jj * (1 - core) + ii * core
        return zz * 2 + xx, yy

    def rows_of(sec):
        return pl.ds(pl.multiple_of(sec * rows, rows), rows)

    def device(zz, ii, jj):
        sec, yy = place(zz, ii, jj)
        return sec, yy * 2 + core

    a_dev = device(z, i, 1 - j)
    b_dev = device(z, 1 - i, j)
    sib_dev = (section, py * 2 + 1 - core)
    z_devs = [(flip(z, k) * 2 + px, expert) for k in range(1, depth)]

    own_block = x.at[expert, rows_of(section)]
    tok_load = pltpu.make_async_copy(tok, own_block, load_sem.at[0])
    tok_load.start()
    loads = [
        pltpu.make_async_copy(gains, gains_v, load_sem.at[1]),
        pltpu.make_async_copy(ids, ids_v, load_sem.at[2]),
        pltpu.make_async_copy(ints, ints_v, load_sem.at[3]),
    ]
    for e in range(x.shape[0]):
        part = pl.ds(e * width, width)
        for n, w in enumerate((wg, wu)):
            loads.append(
                pltpu.make_async_copy(
                    w.at[0, part], w_in.at[part, pl.ds(n * hid, hid)], load_sem.at[4 + 2 * e + n]
                )
            )

    def wd_slice(e):
        return wd.at[0, :, pl.ds(pl.multiple_of(e * width, width), width)]

    out_loads = [
        pltpu.make_async_copy(
            wd_slice(yy * 2 + core), w_out.at[0, yy], load_sem.at[4 + 2 * x.shape[0] + yy]
        )
        for yy in range(2)
    ]
    barrier = pltpu.get_barrier_semaphore()
    partners = z_devs + [a_dev, b_dev, sib_dev]
    for partner in partners:
        pl.semaphore_signal(barrier, inc=1, device_id=partner, device_id_type=MESH)
    for load in loads + out_loads:
        load.start()
    pl.semaphore_wait(barrier, len(partners))
    tok_load.wait()

    pending = []

    def block(zz, ii, jj):
        sec, yy = place(zz, ii, jj)
        return x.at[yy * 2 + core, rows_of(sec)]

    def push(source, zz, ii, jj, send_sem, target):
        copy = pltpu.make_async_remote_copy(
            src_ref=source, dst_ref=block(zz, ii, jj), send_sem=send_sem,
            recv_sem=in_recv.at[(zz * 2 + ii) * 2 + jj],
            device_id=target, device_id_type=MESH,
        )
        copy.start()
        pending.append(copy)

    def push_sib(source, zz, ii, jj):
        sec, yy = place(zz, ii, jj)
        copy = pltpu.make_async_remote_copy(
            src_ref=source, dst_ref=block(zz, ii, jj), send_sem=in_sib_send.at[sec * 2 + yy],
            recv_sem=in_sib_recv.at[sec * 2 + yy],
            device_id=sib_dev, device_id_type=MESH,
        )
        copy.start()
        pending.append(copy)

    def arrived(zz, ii, jj):
        here = block(zz, ii, jj)
        pltpu.make_async_remote_copy(
            src_ref=here, dst_ref=here, send_sem=in_z_send.at[0],
            recv_sem=in_recv.at[(zz * 2 + ii) * 2 + jj],
            device_id=sib_dev, device_id_type=MESH,
        ).wait_recv()
        return here

    for k in range(1, depth):
        push(own_block, z, i, j, in_z_send.at[k - 1], z_devs[k - 1])
    push(own_block, z, i, j, in_a_send.at[0], a_dev)
    push(own_block, z, i, j, in_b_send.at[0], b_dev)
    push_sib(own_block, z, i, j)
    w_copies = [
        pltpu.make_async_remote_copy(
            src_ref=wd_slice(yy * 2 + 1 - core), dst_ref=w_out.at[1, yy],
            send_sem=w_send.at[yy], recv_sem=w_recv.at[yy],
            device_id=sib_dev, device_id_type=MESH,
        )
        for yy in range(2)
    ]
    for copy in w_copies:
        copy.start()
        pending.append(copy)
    for k in range(1, depth):
        zz = flip(z, k)
        here = arrived(zz, i, j)
        push(here, zz, i, j, in_a_send.at[k], a_dev)
        push(here, zz, i, j, in_b_send.at[k], b_dev)
        push_sib(here, zz, i, j)
    for k in range(depth):
        zz = flip(z, k)
        here = arrived(zz, i, 1 - j)
        push(here, zz, i, 1 - j, in_b_send.at[depth + k], b_dev)
        push_sib(here, zz, i, 1 - j)

    def tiles(body):
        if total == TILE:
            body(pl.ds(0, TILE))
        else:
            @pl.loop(0, total // TILE)
            def _(t):
                body(pl.ds(pl.multiple_of(t * TILE, TILE), TILE))

    def project(e, first):
        def one(span):
            squares = jnp.zeros((TILE, LANES), F32) if first else ss[span]
            for c in range(0, width, LANES):
                cols = pl.ds(c, LANES)
                part = x[e, span, cols].astype(F32)
                squares = squares + part * part
                xn[:, cols] = (part * gains_v[e, :, cols]).astype(BF16)
            ss[span] = squares
            product = jnp.dot(
                xn[...], w_in[pl.ds(pl.multiple_of(e * width, width), width)],
                preferred_element_type=F32,
            )
            acc[span] = product if first else acc[span] + product
        tiles(one)

    def forward(jj, ks):
        for k in ks:
            zz = flip(z, k)
            push_sib(arrived(zz, 1 - i, jj), zz, 1 - i, jj)

    def sib_slice(yy):
        for sec in range(2 * depth):
            here = x.at[yy * 2 + 1 - core, rows_of(sec)]
            pltpu.make_async_remote_copy(
                src_ref=here, dst_ref=here, send_sem=in_z_send.at[0],
                recv_sem=in_sib_recv.at[sec * 2 + yy],
                device_id=sib_dev, device_id_type=MESH,
            ).wait_recv()

    forward(j, range(depth))
    for load in loads:
        load.wait()
    for n, which in enumerate((expert, py * 2 + 1 - core)):
        chosen = jnp.where(ids_v[...] == which, ints_v[...].astype(F32) / 65536.0, 0.0)
        row = jnp.sum(chosen, axis=0, keepdims=True)
        weight[n] = jnp.broadcast_to(row, (8, total)).T[:, :1]
    project(py * 2 + core, True)
    forward(1 - j, range(depth // 2))
    sib_slice(py)
    project(py * 2 + 1 - core, False)
    forward(1 - j, range(depth // 2, depth))
    project((1 - py) * 2 + core, False)
    sib_slice(1 - py)
    project((1 - py) * 2 + 1 - core, False)

    def activate(span):
        mean_sq = jnp.sum(ss[span], axis=-1, keepdims=True) / features
        both = acc[span] * lax.rsqrt(mean_sq + EPS)
        gate, up = both[:, :hid], both[:, hid:]
        inner[0, span] = (gate / (1.0 + jnp.exp(-gate)) * up).astype(BF16)

    tiles(activate)

    inner_copy = pltpu.make_async_remote_copy(
        src_ref=inner.at[0], dst_ref=inner.at[1], send_sem=inner_send, recv_sem=inner_recv,
        device_id=sib_dev, device_id_type=MESH,
    )
    inner_copy.start()
    pending.append(inner_copy)

    def down(yy, n):
        def one(span):
            product = (
                jnp.dot(inner[n, span], w_out[n, yy], preferred_element_type=F32) * weight[n, span]
            )
            own[yy, span] = own[yy, span] + product if n else product
        tiles(one)

    for load in out_loads:
        load.wait()
    for yy in (1 - py, py):
        down(yy, 0)
    for copy in w_copies:
        copy.wait_recv()
    inner_copy.wait_recv()

    def mine(zz, ii, jj):
        sec, yy = place(zz, ii, jj)
        span = rows_of(sec)
        return own[yy, span]

    def send(value, source, source_slot, target, target_slot, send_sem, recv_sem, dev):
        source[source_slot] = value.astype(BF16)
        copy = pltpu.make_async_remote_copy(
            src_ref=source.at[source_slot], dst_ref=target.at[target_slot],
            send_sem=send_sem.at[source_slot], recv_sem=recv_sem.at[target_slot],
            device_id=dev, device_id_type=MESH,
        )
        copy.start()
        pending.append(copy)

    def take(target, slot, recv_sem):
        pltpu.make_async_remote_copy(
            src_ref=target.at[slot], dst_ref=target.at[slot], send_sem=in_z_send.at[0],
            recv_sem=recv_sem.at[slot], device_id=sib_dev, device_id_type=MESH,
        ).wait_recv()
        return target[slot].astype(F32)

    order = list(range(1, depth)) + [0]
    for yy, jj in ((1 - py, 1 - j), (py, j)):
        down(yy, 1)
        for k in order:
            zz = flip(z, k)
            slot = jj * depth + zz
            send(mine(zz, 1 - i, jj), b_s, slot, b_r, slot, b_send, b_recv, b_dev)
    for k in order:
        zz = flip(z, k)
        value = mine(zz, i, 1 - j) + take(b_r, (1 - j) * depth + zz, b_recv)
        send(value, a_s, zz, a_r, zz, a_send, a_recv, a_dev)
    for k in order:
        zz = flip(z, k)
        value = mine(zz, i, j) + take(b_r, j * depth + zz, b_recv) + take(a_r, zz, a_recv)
        if k:
            send(value, z_s, zz, z_r, z, z_send, z_recv, z_devs[k - 1])
    for k in range(1, depth):
        value = value + take(z_r, flip(z, k), z_recv)
    out[...] = (x[expert, rows_of(section)].astype(F32) + value).astype(BF16)
    for copy in pending:
        copy.wait_send()


def body(tokens, gains, w_gate, w_up, w_down, expert_ids, gate_ints, *, sections, experts):
    rows, width = tokens.shape
    hid = w_gate.shape[2]
    features = gains.shape[0]
    total = expert_ids.shape[0]
    top = expert_ids.shape[1]
    depth = sections // 2
    dma = pltpu.SemaphoreType.DMA
    blocks = 4 * depth
    return pl.pallas_call(
        functools.partial(kernel, depth),
        out_shape=jax.ShapeDtypeStruct((rows, width), BF16),
        in_specs=[pl.BlockSpec(memory_space=pl.ANY)] * 7,
        out_specs=pl.BlockSpec(memory_space=pltpu.VMEM),
        scratch_shapes=[
            pltpu.VMEM((experts, total, width), BF16),
            pltpu.VMEM((TILE, width), BF16),
            pltpu.VMEM((features, 2 * hid), BF16),
            pltpu.VMEM((2, 2, hid, width), BF16),
            pltpu.VMEM((experts, 1, width), F32),
            pltpu.VMEM((top, total), jnp.int32),
            pltpu.VMEM((top, total), jnp.int32),
            pltpu.VMEM((2, total, hid), BF16),
            pltpu.VMEM((2, total, 1), F32),
            pltpu.VMEM((total, LANES), F32),
            pltpu.VMEM((total, 2 * hid), F32),
            pltpu.VMEM((2, total, width), F32),
            pltpu.VMEM((2 * depth, rows, width), BF16),
            pltpu.VMEM((2 * depth, rows, width), BF16),
            pltpu.VMEM((depth, rows, width), BF16),
            pltpu.VMEM((depth, rows, width), BF16),
            pltpu.VMEM((depth, rows, width), BF16),
            pltpu.VMEM((depth, rows, width), BF16),
            dma((6 + 2 * experts,)),
            dma((blocks,)), dma((blocks,)),
            dma((depth,)), dma((depth,)), dma((2 * depth,)), dma((blocks,)),
            dma((2,)), dma((2,)), dma, dma,
            dma((2 * depth,)), dma((2 * depth,)),
            dma((depth,)), dma((depth,)),
            dma((depth,)), dma((depth,)),
        ],
        compiler_params=pltpu.CompilerParams(
            collective_id=0, has_side_effects=True, vmem_limit_bytes=62 * 1024 * 1024,
        ),
    )(tokens, gains.reshape(experts, 1, width), w_gate, w_up, w_down, expert_ids.T, gate_ints.T)


def solution(mesh):
    in_specs = (
        P("section", "expert"),
        P(),
        P("expert", None, "section"),
        P("expert", None, "section"),
        P("expert", "section", None),
        P(),
        P(),
    )
    run = functools.partial(
        body, sections=mesh.shape["section"], experts=mesh.shape["expert"]
    )
    return jax.shard_map(
        run, mesh=mesh, in_specs=in_specs, out_specs=P("section", "expert"), check_vma=False
    )
```

```python
import functools

import jax
import jax.numpy as jnp
from jax import lax
from jax.experimental import pallas as pl
from jax.experimental.pallas import tpu as pltpu
from jax.sharding import PartitionSpec as P

EPS = 1e-05
MESH = pl.DeviceIdType.MESH
BF16 = jnp.bfloat16
F32 = jnp.float32
TILE = 128
LANES = 128


def flip(index, mask):
    bit = 1
    while bit <= mask:
        if mask & bit:
            index = index + bit - 2 * bit * lax.rem(lax.div(index, bit), 2)
        bit *= 2
    return index


def kernel(
    depth, tok, gains, wg, wu, wd, ids, ints, out,
    x, xn, w_in, w_out, gains_v, ids_v, ints_v, inner, weight, ss, acc,
    own, b_s, b_r, a_s, a_r, z_s, z_r,
    load_sem, in_recv, in_sib_recv, in_z_send, in_a_send, in_b_send, in_sib_send,
    w_send, w_recv, inner_send, inner_recv, b_send, b_recv, a_send, a_recv, z_send, z_recv,
):
    section, expert = lax.axis_index("section"), lax.axis_index("expert")
    z, px = lax.div(section, 2), lax.rem(section, 2)
    py, core = lax.div(expert, 2), lax.rem(expert, 2)
    rows, width = tok.shape
    total = x.shape[1]
    hid = wg.shape[2]
    features = x.shape[0] * width
    i = py * (1 - core) + px * core
    j = px * (1 - core) + py * core

    def place(zz, ii, jj):
        yy = ii * (1 - core) + jj * core
        xx = jj * (1 - core) + ii * core
        return xx, yy

    def spot(zz, xx, count=1):
        return pl.ds(pl.multiple_of((xx * depth + zz) * rows, rows), count * rows)

    def device(zz, ii, jj):
        xx, yy = place(zz, ii, jj)
        return zz * 2 + xx, yy * 2 + core

    a_dev = device(z, i, 1 - j)
    b_dev = device(z, 1 - i, j)
    sib_dev = (section, py * 2 + 1 - core)
    z_devs = [(flip(z, k) * 2 + px, expert) for k in range(1, depth)]

    own_block = x.at[expert, spot(z, px)]
    tok_load = pltpu.make_async_copy(tok, own_block, load_sem.at[0])
    tok_load.start()
    loads = [
        pltpu.make_async_copy(gains, gains_v, load_sem.at[1]),
        pltpu.make_async_copy(ids, ids_v, load_sem.at[2]),
        pltpu.make_async_copy(ints, ints_v, load_sem.at[3]),
    ]
    for e in range(x.shape[0]):
        part = pl.ds(e * width, width)
        for n, w in enumerate((wg, wu)):
            loads.append(
                pltpu.make_async_copy(
                    w.at[0, part], w_in.at[part, pl.ds(n * hid, hid)], load_sem.at[4 + 2 * e + n]
                )
            )

    def wd_slice(e):
        return wd.at[0, :, pl.ds(pl.multiple_of(e * width, width), width)]

    out_loads = [
        pltpu.make_async_copy(
            wd_slice(yy * 2 + core), w_out.at[0, yy], load_sem.at[4 + 2 * x.shape[0] + yy]
        )
        for yy in range(2)
    ]
    barrier = pltpu.get_barrier_semaphore()
    partners = z_devs + [a_dev, b_dev, sib_dev]
    for partner in partners:
        pl.semaphore_signal(barrier, inc=1, device_id=partner, device_id_type=MESH)
    for load in loads + out_loads:
        load.start()
    pl.semaphore_wait(barrier, len(partners))
    tok_load.wait()

    def block(zz, ii, jj):
        xx, yy = place(zz, ii, jj)
        return x.at[yy * 2 + core, spot(zz, xx)]

    def push(source, zz, ii, jj, send_sem, target):
        pltpu.make_async_remote_copy(
            src_ref=source, dst_ref=block(zz, ii, jj), send_sem=send_sem,
            recv_sem=in_recv.at[(zz * 2 + ii) * 2 + jj],
            device_id=target, device_id_type=MESH,
        ).start()

    def push_sib(ii, jj, first, count):
        xx, yy = place(z, ii, jj)
        here = x.at[yy * 2 + core, spot(first, xx, count)]
        pltpu.make_async_remote_copy(
            src_ref=here, dst_ref=here, send_sem=in_sib_send, recv_sem=in_sib_recv.at[yy],
            device_id=sib_dev, device_id_type=MESH,
        ).start()

    def wait_recv(ref, sem):
        pltpu.make_async_remote_copy(
            src_ref=ref, dst_ref=ref, send_sem=in_z_send, recv_sem=sem,
            device_id=sib_dev, device_id_type=MESH,
        ).wait_recv()

    def wait_send(ref, sem):
        pltpu.make_async_remote_copy(
            src_ref=ref, dst_ref=ref, send_sem=sem, recv_sem=in_recv.at[0],
            device_id=sib_dev, device_id_type=MESH,
        ).wait_send()

    def arrived(zz, ii, jj):
        here = block(zz, ii, jj)
        wait_recv(here, in_recv.at[(zz * 2 + ii) * 2 + jj])
        return here

    for k in range(1, depth):
        push(own_block, z, i, j, in_z_send, z_devs[k - 1])
    push(own_block, z, i, j, in_a_send, a_dev)
    push(own_block, z, i, j, in_b_send, b_dev)
    w_copies = [
        pltpu.make_async_remote_copy(
            src_ref=wd_slice(yy * 2 + 1 - core), dst_ref=w_out.at[1, yy],
            send_sem=w_send.at[yy], recv_sem=w_recv.at[yy],
            device_id=sib_dev, device_id_type=MESH,
        )
        for yy in range(2)
    ]
    for copy in w_copies:
        copy.start()
    for k in range(1, depth):
        zz = flip(z, k)
        here = arrived(zz, i, j)
        push(here, zz, i, j, in_a_send, a_dev)
        push(here, zz, i, j, in_b_send, b_dev)
    push_sib(i, j, 0, depth)
    for k in range(depth):
        zz = flip(z, k)
        push(arrived(zz, i, 1 - j), zz, i, 1 - j, in_b_send, b_dev)
    push_sib(i, 1 - j, 0, depth)

    def tiles(body):
        if total == TILE:
            body(pl.ds(0, TILE))
        else:
            @pl.loop(0, total // TILE)
            def _(t):
                body(pl.ds(pl.multiple_of(t * TILE, TILE), TILE))

    def project(e, first):
        def one(span):
            squares = jnp.zeros((TILE, LANES), F32) if first else ss[span]
            for c in range(0, width, LANES):
                cols = pl.ds(c, LANES)
                part = x[e, span, cols].astype(F32)
                squares = squares + part * part
                xn[:, cols] = (part * gains_v[e, :, cols]).astype(BF16)
            ss[span] = squares
            product = jnp.dot(
                xn[...], w_in[pl.ds(pl.multiple_of(e * width, width), width)],
                preferred_element_type=F32,
            )
            acc[span] = product if first else acc[span] + product
        tiles(one)

    half = depth // 2

    def forward(jj, ks, first):
        for k in ks:
            arrived(flip(z, k), 1 - i, jj)
        push_sib(1 - i, jj, first, len(ks))

    def sib_slice(yy):
        wait_recv(x.at[yy * 2 + 1 - core], in_sib_recv.at[yy])

    forward(j, range(depth), 0)
    for load in loads:
        load.wait()
    for n, which in enumerate((expert, py * 2 + 1 - core)):
        chosen = jnp.where(ids_v[...] == which, ints_v[...].astype(F32) / 65536.0, 0.0)
        row = jnp.sum(chosen, axis=0, keepdims=True)
        column = jnp.broadcast_to(row, (8, total)).T[:, :1]
        for sec in range(2 * depth):
            weight[n, spot(sec // 2, sec % 2)] = column[sec * rows : (sec + 1) * rows]
    project(py * 2 + core, True)
    forward(1 - j, range(half), lax.div(z, half) * half)
    sib_slice(py)
    project(py * 2 + 1 - core, False)
    forward(1 - j, range(half, depth), half - lax.div(z, half) * half)
    project((1 - py) * 2 + core, False)
    sib_slice(1 - py)
    project((1 - py) * 2 + 1 - core, False)

    def activate(span):
        mean_sq = jnp.sum(ss[span], axis=-1, keepdims=True) / features
        both = acc[span] * lax.rsqrt(mean_sq + EPS)
        gate, up = both[:, :hid], both[:, hid:]
        inner[0, span] = (gate / (1.0 + jnp.exp(-gate)) * up).astype(BF16)

    tiles(activate)

    inner_copy = pltpu.make_async_remote_copy(
        src_ref=inner.at[0], dst_ref=inner.at[1], send_sem=inner_send, recv_sem=inner_recv,
        device_id=sib_dev, device_id_type=MESH,
    )
    inner_copy.start()

    def down(yy, n):
        def one(span):
            product = (
                jnp.dot(inner[n, span], w_out[n, yy], preferred_element_type=F32) * weight[n, span]
            )
            own[yy, span] = own[yy, span] + product if n else product
        tiles(one)

    for load in out_loads:
        load.wait()
    for yy in (1 - py, py):
        down(yy, 0)
    for copy in w_copies:
        copy.wait_recv()
    inner_copy.wait_recv()

    def mine(zz, ii, jj):
        xx, yy = place(zz, ii, jj)
        return own[yy, spot(zz, xx)]

    def send(value, source, target, slot, send_sem, recv_sem, dev):
        source[slot] = value.astype(BF16)
        pltpu.make_async_remote_copy(
            src_ref=source.at[slot], dst_ref=target.at[slot], send_sem=send_sem,
            recv_sem=recv_sem, device_id=dev, device_id_type=MESH,
        ).start()

    def take(target, slot, recv_sem):
        wait_recv(target.at[slot], recv_sem.at[slot])
        return target[slot].astype(F32)

    order = list(range(1, depth)) + [0]
    for yy, jj in ((1 - py, 1 - j), (py, j)):
        down(yy, 1)
        for k in order:
            zz = flip(z, k)
            slot = jj * depth + zz
            send(mine(zz, 1 - i, jj), b_s, b_r, slot, b_send, b_recv.at[slot], b_dev)
    wait_send(x.at[0, pl.ds(0, (depth - 1) * rows)], in_z_send)
    wait_send(x.at[0, pl.ds(0, depth * rows)], in_a_send)
    wait_send(x.at[0], in_b_send)
    wait_send(x.at[pl.ds(0, 2)], in_sib_send)
    for copy in w_copies + [inner_copy]:
        copy.wait_send()
    for k in order:
        zz = flip(z, k)
        value = mine(zz, i, 1 - j) + take(b_r, (1 - j) * depth + zz, b_recv)
        send(value, a_s, a_r, zz, a_send, a_recv.at[zz], a_dev)
    for k in order:
        zz = flip(z, k)
        value = mine(zz, i, j) + take(b_r, j * depth + zz, b_recv) + take(a_r, zz, a_recv)
        if k:
            send(value, z_s, z_r, k - 1, z_send, z_recv, z_devs[k - 1])
    value = value + x[expert, spot(z, px)].astype(F32)
    wait_send(b_s, b_send)
    wait_send(a_s, a_send)
    wait_recv(z_r, z_recv)
    for k in range(1, depth):
        value = value + z_r[k - 1].astype(F32)
    out[...] = value.astype(BF16)
    wait_send(z_s, z_send)


def body(tokens, gains, w_gate, w_up, w_down, expert_ids, gate_ints, *, sections, experts):
    rows, width = tokens.shape
    hid = w_gate.shape[2]
    features = gains.shape[0]
    total = expert_ids.shape[0]
    top = expert_ids.shape[1]
    depth = sections // 2
    dma = pltpu.SemaphoreType.DMA
    blocks = 4 * depth
    return pl.pallas_call(
        functools.partial(kernel, depth),
        out_shape=jax.ShapeDtypeStruct((rows, width), BF16),
        in_specs=[pl.BlockSpec(memory_space=pl.ANY)] * 7,
        out_specs=pl.BlockSpec(memory_space=pltpu.VMEM),
        scratch_shapes=[
            pltpu.VMEM((experts, total, width), BF16),
            pltpu.VMEM((TILE, width), BF16),
            pltpu.VMEM((features, 2 * hid), BF16),
            pltpu.VMEM((2, 2, hid, width), BF16),
            pltpu.VMEM((experts, 1, width), F32),
            pltpu.VMEM((top, total), jnp.int32),
            pltpu.VMEM((top, total), jnp.int32),
            pltpu.VMEM((2, total, hid), BF16),
            pltpu.VMEM((2, total, 1), F32),
            pltpu.VMEM((total, LANES), F32),
            pltpu.VMEM((total, 2 * hid), F32),
            pltpu.VMEM((2, total, width), F32),
            pltpu.VMEM((2 * depth, rows, width), BF16),
            pltpu.VMEM((2 * depth, rows, width), BF16),
            pltpu.VMEM((depth, rows, width), BF16),
            pltpu.VMEM((depth, rows, width), BF16),
            pltpu.VMEM((depth - 1, rows, width), BF16),
            pltpu.VMEM((depth - 1, rows, width), BF16),
            dma((6 + 2 * experts,)),
            dma((blocks,)), dma((2,)), dma, dma, dma, dma,
            dma((2,)), dma((2,)), dma, dma,
            dma, dma((2 * depth,)),
            dma, dma((depth,)),
            dma, dma,
        ],
        compiler_params=pltpu.CompilerParams(
            collective_id=0, has_side_effects=True, vmem_limit_bytes=62 * 1024 * 1024,
        ),
    )(tokens, gains.reshape(experts, 1, width), w_gate, w_up, w_down, expert_ids.T, gate_ints.T)


def solution(mesh):
    in_specs = (
        P("section", "expert"),
        P(),
        P("expert", None, "section"),
        P("expert", None, "section"),
        P("expert", "section", None),
        P(),
        P(),
    )
    run = functools.partial(
        body, sections=mesh.shape["section"], experts=mesh.shape["expert"]
    )
    return jax.shard_map(
        run, mesh=mesh, in_specs=in_specs, out_specs=P("section", "expert"), check_vma=False
    )
```

```python
import functools

import jax
import jax.numpy as jnp
from jax import lax
from jax.experimental import pallas as pl
from jax.experimental.pallas import tpu as pltpu
from jax.sharding import PartitionSpec as P

EPS = 1e-05
MESH = pl.DeviceIdType.MESH
BF16 = jnp.bfloat16
F32 = jnp.float32
TILE = 128
LANES = 128


def flip(index, mask):
    bit = 1
    while bit <= mask:
        if mask & bit:
            index = index + bit - 2 * bit * lax.rem(lax.div(index, bit), 2)
        bit *= 2
    return index


def kernel(
    depth, tok, gains, wg, wu, wd, ids, ints, out,
    x, xn, w_in, w_out, gains_v, ids_v, ints_v, inner, weight, ss, acc,
    own, b_s, b_r, a_s, a_r, z_s, z_r,
    load_sem, in_recv, in_sib_recv, in_z_send, in_a_send, in_b_send, in_sib_send,
    w_send, w_recv, inner_send, inner_recv, b_send, b_recv, a_send, a_recv, z_send, z_recv,
):
    section, expert = lax.axis_index("section"), lax.axis_index("expert")
    z, px = lax.div(section, 2), lax.rem(section, 2)
    py, core = lax.div(expert, 2), lax.rem(expert, 2)
    rows, width = tok.shape
    total = x.shape[1]
    hid = wg.shape[2]
    features = x.shape[0] * width
    i = py * (1 - core) + px * core
    j = px * (1 - core) + py * core

    def place(zz, ii, jj):
        yy = ii * (1 - core) + jj * core
        xx = jj * (1 - core) + ii * core
        return xx, yy

    def spot(zz, xx, count=1):
        return pl.ds(pl.multiple_of((xx * depth + zz) * rows, rows), count * rows)

    def device(zz, ii, jj):
        xx, yy = place(zz, ii, jj)
        return zz * 2 + xx, yy * 2 + core

    a_dev = device(z, i, 1 - j)
    b_dev = device(z, 1 - i, j)
    sib_dev = (section, py * 2 + 1 - core)
    z_devs = [(flip(z, k) * 2 + px, expert) for k in range(1, depth)]

    own_block = x.at[expert, spot(z, px)]
    tok_load = pltpu.make_async_copy(tok, own_block, load_sem.at[0])
    tok_load.start()
    loads = [
        pltpu.make_async_copy(gains, gains_v, load_sem.at[1]),
        pltpu.make_async_copy(ids, ids_v, load_sem.at[2]),
        pltpu.make_async_copy(ints, ints_v, load_sem.at[3]),
    ]
    for e in range(x.shape[0]):
        part = pl.ds(e * width, width)
        for n, w in enumerate((wg, wu)):
            loads.append(
                pltpu.make_async_copy(
                    w.at[0, part], w_in.at[part, pl.ds(n * hid, hid)], load_sem.at[4 + 2 * e + n]
                )
            )

    def wd_slice(e):
        return wd.at[0, :, pl.ds(pl.multiple_of(e * width, width), width)]

    out_loads = [
        pltpu.make_async_copy(
            wd_slice(yy * 2 + core), w_out.at[0, yy], load_sem.at[4 + 2 * x.shape[0] + yy]
        )
        for yy in range(2)
    ]
    barrier = pltpu.get_barrier_semaphore()
    plane = z_devs + [a_dev, b_dev]
    for partner in plane:
        pl.semaphore_signal(barrier, inc=1, device_id=partner, device_id_type=MESH)
    for load in loads + out_loads:
        load.start()

    def greet_sib():
        pl.semaphore_signal(barrier, inc=1, device_id=sib_dev, device_id_type=MESH)

    @pl.when(core == 0)
    def _():
        pl.semaphore_wait(barrier, len(plane))
        greet_sib()

    @pl.when(core == 1)
    def _():
        pl.semaphore_wait(barrier, len(plane) + 1)
        greet_sib()

    tok_load.wait()

    def block(zz, ii, jj):
        xx, yy = place(zz, ii, jj)
        return x.at[yy * 2 + core, spot(zz, xx)]

    def push(source, zz, ii, jj, send_sem, target):
        pltpu.make_async_remote_copy(
            src_ref=source, dst_ref=block(zz, ii, jj), send_sem=send_sem,
            recv_sem=in_recv.at[(zz * 2 + ii) * 2 + jj],
            device_id=target, device_id_type=MESH,
        ).start()

    def push_sib(ii, jj, first, count):
        xx, yy = place(z, ii, jj)
        here = x.at[yy * 2 + core, spot(first, xx, count)]
        pltpu.make_async_remote_copy(
            src_ref=here, dst_ref=here, send_sem=in_sib_send, recv_sem=in_sib_recv.at[yy],
            device_id=sib_dev, device_id_type=MESH,
        ).start()

    def wait_recv(ref, sem):
        pltpu.make_async_remote_copy(
            src_ref=ref, dst_ref=ref, send_sem=in_z_send, recv_sem=sem,
            device_id=sib_dev, device_id_type=MESH,
        ).wait_recv()

    def wait_send(ref, sem):
        pltpu.make_async_remote_copy(
            src_ref=ref, dst_ref=ref, send_sem=sem, recv_sem=in_recv.at[0],
            device_id=sib_dev, device_id_type=MESH,
        ).wait_send()

    def arrived(zz, ii, jj):
        here = block(zz, ii, jj)
        wait_recv(here, in_recv.at[(zz * 2 + ii) * 2 + jj])
        return here

    for k in range(1, depth):
        push(own_block, z, i, j, in_z_send, z_devs[k - 1])
    push(own_block, z, i, j, in_a_send, a_dev)
    push(own_block, z, i, j, in_b_send, b_dev)
    w_copies = [
        pltpu.make_async_remote_copy(
            src_ref=wd_slice(yy * 2 + 1 - core), dst_ref=w_out.at[1, yy],
            send_sem=w_send.at[yy], recv_sem=w_recv.at[yy],
            device_id=sib_dev, device_id_type=MESH,
        )
        for yy in range(2)
    ]
    for k in range(1, depth):
        zz = flip(z, k)
        here = arrived(zz, i, j)
        push(here, zz, i, j, in_a_send, a_dev)
        push(here, zz, i, j, in_b_send, b_dev)

    @pl.when(core == 0)
    def _():
        pl.semaphore_wait(barrier, 1)

    for copy in w_copies:
        copy.start()
    push_sib(i, j, 0, depth)
    for k in range(depth):
        zz = flip(z, k)
        push(arrived(zz, i, 1 - j), zz, i, 1 - j, in_b_send, b_dev)
    push_sib(i, 1 - j, 0, depth)

    def tiles(body):
        if total == TILE:
            body(pl.ds(0, TILE))
        else:
            @pl.loop(0, total // TILE)
            def _(t):
                body(pl.ds(pl.multiple_of(t * TILE, TILE), TILE))

    def project(e, first):
        def one(span):
            squares = jnp.zeros((TILE, LANES), F32) if first else ss[span]
            for c in range(0, width, LANES):
                cols = pl.ds(c, LANES)
                part = x[e, span, cols].astype(F32)
                squares = squares + part * part
                xn[:, cols] = (part * gains_v[e, :, cols]).astype(BF16)
            ss[span] = squares
            product = jnp.dot(
                xn[...], w_in[pl.ds(pl.multiple_of(e * width, width), width)],
                preferred_element_type=F32,
            )
            acc[span] = product if first else acc[span] + product
        tiles(one)

    half = depth // 2

    def forward(jj, ks, first):
        for k in ks:
            arrived(flip(z, k), 1 - i, jj)
        push_sib(1 - i, jj, first, len(ks))

    def sib_slice(yy):
        wait_recv(x.at[yy * 2 + 1 - core], in_sib_recv.at[yy])

    forward(j, range(depth), 0)
    for load in loads:
        load.wait()
    for n, which in enumerate((expert, py * 2 + 1 - core)):
        chosen = jnp.where(ids_v[...] == which, ints_v[...].astype(F32) / 65536.0, 0.0)
        row = jnp.sum(chosen, axis=0, keepdims=True)
        column = jnp.broadcast_to(row, (8, total)).T[:, :1]
        for sec in range(2 * depth):
            weight[n, spot(sec // 2, sec % 2)] = column[sec * rows : (sec + 1) * rows]
    project(py * 2 + core, True)
    forward(1 - j, range(half), lax.div(z, half) * half)
    sib_slice(py)
    project(py * 2 + 1 - core, False)
    forward(1 - j, range(half, depth), half - lax.div(z, half) * half)
    project((1 - py) * 2 + core, False)
    sib_slice(1 - py)
    project((1 - py) * 2 + 1 - core, False)

    def activate(span):
        mean_sq = jnp.sum(ss[span], axis=-1, keepdims=True) / features
        both = acc[span] * lax.rsqrt(mean_sq + EPS)
        gate, up = both[:, :hid], both[:, hid:]
        inner[0, span] = (gate / (1.0 + jnp.exp(-gate)) * up).astype(BF16)

    tiles(activate)

    inner_copy = pltpu.make_async_remote_copy(
        src_ref=inner.at[0], dst_ref=inner.at[1], send_sem=inner_send, recv_sem=inner_recv,
        device_id=sib_dev, device_id_type=MESH,
    )
    inner_copy.start()

    def down(yy, n):
        def one(span):
            product = (
                jnp.dot(inner[n, span], w_out[n, yy], preferred_element_type=F32) * weight[n, span]
            )
            own[yy, span] = own[yy, span] + product if n else product
        tiles(one)

    for load in out_loads:
        load.wait()
    for yy in (1 - py, py):
        down(yy, 0)
    for copy in w_copies:
        copy.wait_recv()
    inner_copy.wait_recv()

    def mine(zz, ii, jj):
        xx, yy = place(zz, ii, jj)
        return own[yy, spot(zz, xx)]

    def send(value, source, target, slot, send_sem, recv_sem, dev):
        source[slot] = value.astype(BF16)
        pltpu.make_async_remote_copy(
            src_ref=source.at[slot], dst_ref=target.at[slot], send_sem=send_sem,
            recv_sem=recv_sem, device_id=dev, device_id_type=MESH,
        ).start()

    def take(target, slot, recv_sem):
        wait_recv(target.at[slot], recv_sem.at[slot])
        return target[slot].astype(F32)

    order = list(range(1, depth)) + [0]
    for yy, jj in ((1 - py, 1 - j), (py, j)):
        down(yy, 1)
        for k in order:
            zz = flip(z, k)
            slot = jj * depth + zz
            send(mine(zz, 1 - i, jj), b_s, b_r, slot, b_send, b_recv.at[slot], b_dev)
    wait_send(x.at[0, pl.ds(0, (depth - 1) * rows)], in_z_send)
    wait_send(x.at[0, pl.ds(0, depth * rows)], in_a_send)
    wait_send(x.at[0], in_b_send)
    wait_send(x.at[pl.ds(0, 2)], in_sib_send)
    for copy in w_copies + [inner_copy]:
        copy.wait_send()
    for k in order:
        zz = flip(z, k)
        value = mine(zz, i, 1 - j) + take(b_r, (1 - j) * depth + zz, b_recv)
        send(value, a_s, a_r, zz, a_send, a_recv.at[zz], a_dev)
    for k in order:
        zz = flip(z, k)
        value = mine(zz, i, j) + take(b_r, j * depth + zz, b_recv) + take(a_r, zz, a_recv)
        if k:
            send(value, z_s, z_r, k - 1, z_send, z_recv, z_devs[k - 1])
    value = value + x[expert, spot(z, px)].astype(F32)
    wait_send(b_s, b_send)
    wait_send(a_s, a_send)
    wait_recv(z_r, z_recv)
    for k in range(1, depth):
        value = value + z_r[k - 1].astype(F32)
    out[...] = value.astype(BF16)
    wait_send(z_s, z_send)


def body(tokens, gains, w_gate, w_up, w_down, expert_ids, gate_ints, *, sections, experts):
    rows, width = tokens.shape
    hid = w_gate.shape[2]
    features = gains.shape[0]
    total = expert_ids.shape[0]
    top = expert_ids.shape[1]
    depth = sections // 2
    dma = pltpu.SemaphoreType.DMA
    blocks = 4 * depth
    return pl.pallas_call(
        functools.partial(kernel, depth),
        out_shape=jax.ShapeDtypeStruct((rows, width), BF16),
        in_specs=[pl.BlockSpec(memory_space=pl.ANY)] * 7,
        out_specs=pl.BlockSpec(memory_space=pltpu.VMEM),
        scratch_shapes=[
            pltpu.VMEM((experts, total, width), BF16),
            pltpu.VMEM((TILE, width), BF16),
            pltpu.VMEM((features, 2 * hid), BF16),
            pltpu.VMEM((2, 2, hid, width), BF16),
            pltpu.VMEM((experts, 1, width), F32),
            pltpu.VMEM((top, total), jnp.int32),
            pltpu.VMEM((top, total), jnp.int32),
            pltpu.VMEM((2, total, hid), BF16),
            pltpu.VMEM((2, total, 1), F32),
            pltpu.VMEM((total, LANES), F32),
            pltpu.VMEM((total, 2 * hid), F32),
            pltpu.VMEM((2, total, width), F32),
            pltpu.VMEM((2 * depth, rows, width), BF16),
            pltpu.VMEM((2 * depth, rows, width), BF16),
            pltpu.VMEM((depth, rows, width), BF16),
            pltpu.VMEM((depth, rows, width), BF16),
            pltpu.VMEM((depth - 1, rows, width), BF16),
            pltpu.VMEM((depth - 1, rows, width), BF16),
            dma((6 + 2 * experts,)),
            dma((blocks,)), dma((2,)), dma, dma, dma, dma,
            dma((2,)), dma((2,)), dma, dma,
            dma, dma((2 * depth,)),
            dma, dma((depth,)),
            dma, dma,
        ],
        compiler_params=pltpu.CompilerParams(
            collective_id=0, has_side_effects=True, vmem_limit_bytes=62 * 1024 * 1024,
        ),
    )(tokens, gains.reshape(experts, 1, width), w_gate, w_up, w_down, expert_ids.T, gate_ints.T)


def solution(mesh):
    in_specs = (
        P("section", "expert"),
        P(),
        P("expert", None, "section"),
        P("expert", None, "section"),
        P("expert", "section", None),
        P(),
        P(),
    )
    run = functools.partial(
        body, sections=mesh.shape["section"], experts=mesh.shape["expert"]
    )
    return jax.shard_map(
        run, mesh=mesh, in_specs=in_specs, out_specs=P("section", "expert"), check_vma=False
    )
```

```python
import functools

import jax
import jax.numpy as jnp
from jax import lax
from jax.experimental import pallas as pl
from jax.experimental.pallas import tpu as pltpu
from jax.sharding import PartitionSpec as P

EPS = 1e-05
MESH = pl.DeviceIdType.MESH
BF16 = jnp.bfloat16
F32 = jnp.float32
TILE = 128
LANES = 128
PARTS = 2


def flip(index, mask):
    bit = 1
    while bit <= mask:
        if mask & bit:
            index = index + bit - 2 * bit * lax.rem(lax.div(index, bit), 2)
        bit *= 2
    return index


def kernel(
    depth, tok, gains, wg, wu, wd, ids, ints, out,
    x, xn, w_in, w_out, gains_v, ids_v, ints_v, inner, weight, ss, acc,
    own, b_s, b_r, a_s, a_r, z_s, z_r,
    load_sem, in_recv, in_sib_recv, in_z_send, in_a_send, in_b_send, in_sib_send,
    w_send, w_recv, inner_send, inner_recv, b_send, b_recv, a_send, a_recv, z_send, z_recv,
):
    section, expert = lax.axis_index("section"), lax.axis_index("expert")
    z, px = lax.div(section, 2), lax.rem(section, 2)
    py, core = lax.div(expert, 2), lax.rem(expert, 2)
    rows, width = tok.shape
    total = x.shape[1]
    hid = wg.shape[2]
    features = x.shape[0] * width
    i = py * (1 - core) + px * core
    j = px * (1 - core) + py * core

    def place(zz, ii, jj):
        yy = ii * (1 - core) + jj * core
        xx = jj * (1 - core) + ii * core
        return xx, yy

    def spot(zz, xx, count=1):
        return pl.ds(pl.multiple_of((xx * depth + zz) * rows, rows), count * rows)

    def device(zz, ii, jj):
        xx, yy = place(zz, ii, jj)
        return zz * 2 + xx, yy * 2 + core

    a_dev = device(z, i, 1 - j)
    b_dev = device(z, 1 - i, j)
    sib_dev = (section, py * 2 + 1 - core)
    z_devs = [(flip(z, k) * 2 + px, expert) for k in range(1, depth)]

    own_block = x.at[expert, spot(z, px)]
    tok_load = pltpu.make_async_copy(tok, own_block, load_sem.at[0])
    tok_load.start()
    loads = [
        pltpu.make_async_copy(gains, gains_v, load_sem.at[1]),
        pltpu.make_async_copy(ids, ids_v, load_sem.at[2]),
        pltpu.make_async_copy(ints, ints_v, load_sem.at[3]),
    ]
    for e in range(x.shape[0]):
        part = pl.ds(e * width, width)
        for n, w in enumerate((wg, wu)):
            loads.append(
                pltpu.make_async_copy(
                    w.at[0, part], w_in.at[part, pl.ds(n * hid, hid)], load_sem.at[4 + 2 * e + n]
                )
            )

    def wd_slice(e):
        return wd.at[0, :, pl.ds(pl.multiple_of(e * width, width), width)]

    out_loads = [
        pltpu.make_async_copy(
            wd_slice(yy * 2 + core), w_out.at[0, yy], load_sem.at[4 + 2 * x.shape[0] + yy]
        )
        for yy in range(2)
    ]
    barrier = pltpu.get_barrier_semaphore()
    partners = z_devs + [a_dev, b_dev, sib_dev]
    for partner in partners:
        pl.semaphore_signal(barrier, inc=1, device_id=partner, device_id_type=MESH)
    for load in loads + out_loads:
        load.start()
    pl.semaphore_wait(barrier, len(partners))
    tok_load.wait()

    def columns(p):
        return pl.ds(p * (width // PARTS), width // PARTS)

    def block(zz, ii, jj, p):
        xx, yy = place(zz, ii, jj)
        return x.at[yy * 2 + core, spot(zz, xx), columns(p)]

    def mark(zz, ii, jj, p):
        return in_recv.at[((zz * 2 + ii) * 2 + jj) * PARTS + p]

    def push(zz, ii, jj, p, send_sem, target):
        here = block(zz, ii, jj, p)
        pltpu.make_async_remote_copy(
            src_ref=here, dst_ref=here, send_sem=send_sem, recv_sem=mark(zz, ii, jj, p),
            device_id=target, device_id_type=MESH,
        ).start()

    def push_sib(ii, jj, first, count):
        xx, yy = place(z, ii, jj)
        here = x.at[yy * 2 + core, spot(first, xx, count)]
        pltpu.make_async_remote_copy(
            src_ref=here, dst_ref=here, send_sem=in_sib_send, recv_sem=in_sib_recv.at[yy],
            device_id=sib_dev, device_id_type=MESH,
        ).start()

    def wait_recv(ref, sem):
        pltpu.make_async_remote_copy(
            src_ref=ref, dst_ref=ref, send_sem=in_z_send, recv_sem=sem,
            device_id=sib_dev, device_id_type=MESH,
        ).wait_recv()

    def wait_send(ref, sem):
        pltpu.make_async_remote_copy(
            src_ref=ref, dst_ref=ref, send_sem=sem, recv_sem=in_recv.at[0],
            device_id=sib_dev, device_id_type=MESH,
        ).wait_send()

    def arrived(zz, ii, jj, p):
        wait_recv(block(zz, ii, jj, p), mark(zz, ii, jj, p))

    for p in range(PARTS):
        for k in range(1, depth):
            push(z, i, j, p, in_z_send, z_devs[k - 1])
        push(z, i, j, p, in_a_send, a_dev)
        push(z, i, j, p, in_b_send, b_dev)
    w_copies = [
        pltpu.make_async_remote_copy(
            src_ref=wd_slice(yy * 2 + 1 - core), dst_ref=w_out.at[1, yy],
            send_sem=w_send.at[yy], recv_sem=w_recv.at[yy],
            device_id=sib_dev, device_id_type=MESH,
        )
        for yy in range(2)
    ]
    for copy in w_copies:
        copy.start()
    for k in range(1, depth):
        zz = flip(z, k)
        for p in range(PARTS):
            arrived(zz, i, j, p)
            push(zz, i, j, p, in_a_send, a_dev)
            push(zz, i, j, p, in_b_send, b_dev)
    push_sib(i, j, 0, depth)
    for k in range(depth):
        zz = flip(z, k)
        for p in range(PARTS):
            arrived(zz, i, 1 - j, p)
            push(zz, i, 1 - j, p, in_b_send, b_dev)
    push_sib(i, 1 - j, 0, depth)

    def tiles(body):
        if total == TILE:
            body(pl.ds(0, TILE))
        else:
            @pl.loop(0, total // TILE)
            def _(t):
                body(pl.ds(pl.multiple_of(t * TILE, TILE), TILE))

    def project(e, first):
        def one(span):
            squares = jnp.zeros((TILE, LANES), F32) if first else ss[span]
            for c in range(0, width, LANES):
                cols = pl.ds(c, LANES)
                part = x[e, span, cols].astype(F32)
                squares = squares + part * part
                xn[:, cols] = (part * gains_v[e, :, cols]).astype(BF16)
            ss[span] = squares
            product = jnp.dot(
                xn[...], w_in[pl.ds(pl.multiple_of(e * width, width), width)],
                preferred_element_type=F32,
            )
            acc[span] = product if first else acc[span] + product
        tiles(one)

    half = depth // 2

    def forward(jj, ks, first):
        for k in ks:
            for p in range(PARTS):
                arrived(flip(z, k), 1 - i, jj, p)
        push_sib(1 - i, jj, first, len(ks))

    def sib_slice(yy):
        wait_recv(x.at[yy * 2 + 1 - core], in_sib_recv.at[yy])

    forward(j, range(depth), 0)
    for load in loads:
        load.wait()
    for n, which in enumerate((expert, py * 2 + 1 - core)):
        chosen = jnp.where(ids_v[...] == which, ints_v[...].astype(F32) / 65536.0, 0.0)
        row = jnp.sum(chosen, axis=0, keepdims=True)
        column = jnp.broadcast_to(row, (8, total)).T[:, :1]
        for sec in range(2 * depth):
            weight[n, spot(sec // 2, sec % 2)] = column[sec * rows : (sec + 1) * rows]
    project(py * 2 + core, True)
    forward(1 - j, range(half), lax.div(z, half) * half)
    sib_slice(py)
    project(py * 2 + 1 - core, False)
    forward(1 - j, range(half, depth), half - lax.div(z, half) * half)
    project((1 - py) * 2 + core, False)
    sib_slice(1 - py)
    project((1 - py) * 2 + 1 - core, False)

    def activate(span):
        mean_sq = jnp.sum(ss[span], axis=-1, keepdims=True) / features
        both = acc[span] * lax.rsqrt(mean_sq + EPS)
        gate, up = both[:, :hid], both[:, hid:]
        inner[0, span] = (gate / (1.0 + jnp.exp(-gate)) * up).astype(BF16)

    tiles(activate)

    inner_copy = pltpu.make_async_remote_copy(
        src_ref=inner.at[0], dst_ref=inner.at[1], send_sem=inner_send, recv_sem=inner_recv,
        device_id=sib_dev, device_id_type=MESH,
    )
    inner_copy.start()

    def down(yy, n):
        def one(span):
            product = (
                jnp.dot(inner[n, span], w_out[n, yy], preferred_element_type=F32) * weight[n, span]
            )
            own[yy, span] = own[yy, span] + product if n else product
        tiles(one)

    for load in out_loads:
        load.wait()
    for yy in (1 - py, py):
        down(yy, 0)
    for copy in w_copies:
        copy.wait_recv()
    inner_copy.wait_recv()

    def mine(zz, ii, jj, p):
        xx, yy = place(zz, ii, jj)
        return own[yy, spot(zz, xx), columns(p)]

    def send(value, source, target, slot, p, send_sem, recv_sem, dev):
        source[slot, :, columns(p)] = value.astype(BF16)
        pltpu.make_async_remote_copy(
            src_ref=source.at[slot, :, columns(p)], dst_ref=target.at[slot, :, columns(p)],
            send_sem=send_sem, recv_sem=recv_sem, device_id=dev, device_id_type=MESH,
        ).start()

    def take(target, slot, p, recv_sem):
        wait_recv(target.at[slot, :, columns(p)], recv_sem.at[slot * PARTS + p])
        return target[slot, :, columns(p)].astype(F32)

    order = list(range(1, depth)) + [0]
    for yy, jj in ((1 - py, 1 - j), (py, j)):
        down(yy, 1)
        for k in order:
            zz = flip(z, k)
            slot = jj * depth + zz
            for p in range(PARTS):
                send(
                    mine(zz, 1 - i, jj, p), b_s, b_r, slot, p,
                    b_send, b_recv.at[slot * PARTS + p], b_dev,
                )
    wait_send(x.at[0, pl.ds(0, (depth - 1) * rows)], in_z_send)
    wait_send(x.at[0, pl.ds(0, depth * rows)], in_a_send)
    wait_send(x.at[0], in_b_send)
    wait_send(x.at[pl.ds(0, 2)], in_sib_send)
    for copy in w_copies + [inner_copy]:
        copy.wait_send()
    for k in order:
        zz = flip(z, k)
        for p in range(PARTS):
            value = mine(zz, i, 1 - j, p) + take(b_r, (1 - j) * depth + zz, p, b_recv)
            send(value, a_s, a_r, zz, p, a_send, a_recv.at[zz * PARTS + p], a_dev)
    last = []
    for k in order:
        zz = flip(z, k)
        for p in range(PARTS):
            value = (
                mine(zz, i, j, p)
                + take(b_r, j * depth + zz, p, b_recv)
                + take(a_r, zz, p, a_recv)
            )
            if k:
                send(value, z_s, z_r, k - 1, p, z_send, z_recv.at[p], z_devs[k - 1])
            else:
                own_part = x[expert, spot(z, px), columns(p)]
                last.append(value + own_part.astype(F32))
    wait_send(b_s, b_send)
    wait_send(a_s, a_send)
    for p in range(PARTS):
        wait_recv(z_r.at[:, :, columns(p)], z_recv.at[p])
        value = last[p]
        for k in range(1, depth):
            value = value + z_r[k - 1, :, columns(p)].astype(F32)
        out[:, columns(p)] = value.astype(BF16)
    wait_send(z_s, z_send)


def body(tokens, gains, w_gate, w_up, w_down, expert_ids, gate_ints, *, sections, experts):
    rows, width = tokens.shape
    hid = w_gate.shape[2]
    features = gains.shape[0]
    total = expert_ids.shape[0]
    top = expert_ids.shape[1]
    depth = sections // 2
    dma = pltpu.SemaphoreType.DMA
    blocks = 4 * depth
    return pl.pallas_call(
        functools.partial(kernel, depth),
        out_shape=jax.ShapeDtypeStruct((rows, width), BF16),
        in_specs=[pl.BlockSpec(memory_space=pl.ANY)] * 7,
        out_specs=pl.BlockSpec(memory_space=pltpu.VMEM),
        scratch_shapes=[
            pltpu.VMEM((experts, total, width), BF16),
            pltpu.VMEM((TILE, width), BF16),
            pltpu.VMEM((features, 2 * hid), BF16),
            pltpu.VMEM((2, 2, hid, width), BF16),
            pltpu.VMEM((experts, 1, width), F32),
            pltpu.VMEM((top, total), jnp.int32),
            pltpu.VMEM((top, total), jnp.int32),
            pltpu.VMEM((2, total, hid), BF16),
            pltpu.VMEM((2, total, 1), F32),
            pltpu.VMEM((total, LANES), F32),
            pltpu.VMEM((total, 2 * hid), F32),
            pltpu.VMEM((2, total, width), F32),
            pltpu.VMEM((2 * depth, rows, width), BF16),
            pltpu.VMEM((2 * depth, rows, width), BF16),
            pltpu.VMEM((depth, rows, width), BF16),
            pltpu.VMEM((depth, rows, width), BF16),
            pltpu.VMEM((depth - 1, rows, width), BF16),
            pltpu.VMEM((depth - 1, rows, width), BF16),
            dma((6 + 2 * experts,)),
            dma((PARTS * blocks,)), dma((2,)), dma, dma, dma, dma,
            dma((2,)), dma((2,)), dma, dma,
            dma, dma((PARTS * 2 * depth,)),
            dma, dma((PARTS * depth,)),
            dma, dma((PARTS,)),
        ],
        compiler_params=pltpu.CompilerParams(
            collective_id=0, has_side_effects=True, vmem_limit_bytes=62 * 1024 * 1024,
        ),
    )(tokens, gains.reshape(experts, 1, width), w_gate, w_up, w_down, expert_ids.T, gate_ints.T)


def solution(mesh):
    in_specs = (
        P("section", "expert"),
        P(),
        P("expert", None, "section"),
        P("expert", None, "section"),
        P("expert", "section", None),
        P(),
        P(),
    )
    run = functools.partial(
        body, sections=mesh.shape["section"], experts=mesh.shape["expert"]
    )
    return jax.shard_map(
        run, mesh=mesh, in_specs=in_specs, out_specs=P("section", "expert"), check_vma=False
    )
```

```python
import functools

import jax
import jax.numpy as jnp
from jax import lax
from jax.experimental import pallas as pl
from jax.experimental.pallas import tpu as pltpu
from jax.sharding import PartitionSpec as P

EPS = 1e-05
MESH = pl.DeviceIdType.MESH
BF16 = jnp.bfloat16
F32 = jnp.float32
TILE = 128
LANES = 128
PARTS = 2


def flip(index, mask):
    bit = 1
    while bit <= mask:
        if mask & bit:
            index = index + bit - 2 * bit * lax.rem(lax.div(index, bit), 2)
        bit *= 2
    return index


def kernel(
    depth, tok, gains, wg, wu, wd, ids, ints, out,
    x, xn, w_in, w_out, gains_v, ids_v, ints_v, inner, weight, ss, acc,
    own, b_s, b_r, a_s, a_r, z_s, z_r,
    load_sem, in_recv, in_sib_recv, in_z_send, in_a_send, in_b_send, in_sib_send,
    w_send, w_recv, inner_send, inner_recv, b_send, b_recv, a_send, a_recv, z_send, z_recv,
):
    section, expert = lax.axis_index("section"), lax.axis_index("expert")
    z, px = lax.div(section, 2), lax.rem(section, 2)
    py, core = lax.div(expert, 2), lax.rem(expert, 2)
    rows, width = tok.shape
    total = x.shape[1]
    hid = wg.shape[2]
    features = x.shape[0] * width
    i = py * (1 - core) + px * core
    j = px * (1 - core) + py * core

    def place(zz, ii, jj):
        yy = ii * (1 - core) + jj * core
        xx = jj * (1 - core) + ii * core
        return xx, yy

    def spot(zz, xx, count=1):
        return pl.ds(pl.multiple_of((xx * depth + zz) * rows, rows), count * rows)

    def device(zz, ii, jj):
        xx, yy = place(zz, ii, jj)
        return zz * 2 + xx, yy * 2 + core

    a_dev = device(z, i, 1 - j)
    b_dev = device(z, 1 - i, j)
    sib_dev = (section, py * 2 + 1 - core)
    z_devs = [(flip(z, k) * 2 + px, expert) for k in range(1, depth)]

    own_block = x.at[expert, spot(z, px)]
    tok_load = pltpu.make_async_copy(tok, own_block, load_sem.at[0])
    tok_load.start()
    loads = [
        pltpu.make_async_copy(gains, gains_v, load_sem.at[1]),
        pltpu.make_async_copy(ids, ids_v, load_sem.at[2]),
        pltpu.make_async_copy(ints, ints_v, load_sem.at[3]),
    ]
    for e in range(x.shape[0]):
        part = pl.ds(e * width, width)
        for n, w in enumerate((wg, wu)):
            loads.append(
                pltpu.make_async_copy(
                    w.at[0, part], w_in.at[part, pl.ds(n * hid, hid)], load_sem.at[4 + 2 * e + n]
                )
            )

    def wd_slice(e):
        return wd.at[0, :, pl.ds(pl.multiple_of(e * width, width), width)]

    out_loads = [
        pltpu.make_async_copy(
            wd_slice(yy * 2 + core), w_out.at[0, yy], load_sem.at[4 + 2 * x.shape[0] + yy]
        )
        for yy in range(2)
    ]
    barrier = pltpu.get_barrier_semaphore()
    partners = z_devs + [a_dev, b_dev, sib_dev]
    for partner in partners:
        pl.semaphore_signal(barrier, inc=1, device_id=partner, device_id_type=MESH)
    for load in loads + out_loads:
        load.start()
    pl.semaphore_wait(barrier, len(partners))
    tok_load.wait()

    def columns(p):
        return pl.ds(p * (width // PARTS), width // PARTS)

    def block(zz, ii, jj, p):
        xx, yy = place(zz, ii, jj)
        return x.at[yy * 2 + core, spot(zz, xx), columns(p)]

    def mark(zz, ii, jj, p):
        return in_recv.at[((zz * 2 + ii) * 2 + jj) * PARTS + p]

    def push(zz, ii, jj, p, send_sem, target):
        here = block(zz, ii, jj, p)
        pltpu.make_async_remote_copy(
            src_ref=here, dst_ref=here, send_sem=send_sem, recv_sem=mark(zz, ii, jj, p),
            device_id=target, device_id_type=MESH,
        ).start()

    def push_sib(ii, jj, first, count):
        xx, yy = place(z, ii, jj)
        here = x.at[yy * 2 + core, spot(first, xx, count)]
        pltpu.make_async_remote_copy(
            src_ref=here, dst_ref=here, send_sem=in_sib_send, recv_sem=in_sib_recv.at[yy],
            device_id=sib_dev, device_id_type=MESH,
        ).start()

    def wait_recv(ref, sem):
        pltpu.make_async_remote_copy(
            src_ref=ref, dst_ref=ref, send_sem=in_z_send, recv_sem=sem,
            device_id=sib_dev, device_id_type=MESH,
        ).wait_recv()

    def wait_send(ref, sem):
        pltpu.make_async_remote_copy(
            src_ref=ref, dst_ref=ref, send_sem=sem, recv_sem=in_recv.at[0],
            device_id=sib_dev, device_id_type=MESH,
        ).wait_send()

    def arrived(zz, ii, jj, p):
        wait_recv(block(zz, ii, jj, p), mark(zz, ii, jj, p))

    for p in range(PARTS):
        for k in range(1, depth):
            push(z, i, j, p, in_z_send, z_devs[k - 1])
        push(z, i, j, p, in_a_send, a_dev)
        push(z, i, j, p, in_b_send, b_dev)
    w_copies = [
        pltpu.make_async_remote_copy(
            src_ref=wd_slice(yy * 2 + 1 - core), dst_ref=w_out.at[1, yy],
            send_sem=w_send.at[yy], recv_sem=w_recv.at[yy],
            device_id=sib_dev, device_id_type=MESH,
        )
        for yy in range(2)
    ]
    for k in range(1, depth):
        zz = flip(z, k)
        for p in range(PARTS):
            arrived(zz, i, j, p)
            push(zz, i, j, p, in_a_send, a_dev)
            push(zz, i, j, p, in_b_send, b_dev)
    push_sib(i, j, 0, depth)
    for copy in w_copies:
        copy.start()
    for k in range(depth):
        zz = flip(z, k)
        for p in range(PARTS):
            arrived(zz, i, 1 - j, p)
            push(zz, i, 1 - j, p, in_b_send, b_dev)
    push_sib(i, 1 - j, 0, depth)

    def tiles(body):
        if total == TILE:
            body(pl.ds(0, TILE))
        else:
            @pl.loop(0, total // TILE)
            def _(t):
                body(pl.ds(pl.multiple_of(t * TILE, TILE), TILE))

    def project(e, first):
        def one(span):
            squares = jnp.zeros((TILE, LANES), F32) if first else ss[span]
            for c in range(0, width, LANES):
                cols = pl.ds(c, LANES)
                part = x[e, span, cols].astype(F32)
                squares = squares + part * part
                xn[:, cols] = (part * gains_v[e, :, cols]).astype(BF16)
            ss[span] = squares
            product = jnp.dot(
                xn[...], w_in[pl.ds(pl.multiple_of(e * width, width), width)],
                preferred_element_type=F32,
            )
            acc[span] = product if first else acc[span] + product
        tiles(one)

    half = depth // 2

    def forward(jj, ks, first):
        for k in ks:
            for p in range(PARTS):
                arrived(flip(z, k), 1 - i, jj, p)
        push_sib(1 - i, jj, first, len(ks))

    def sib_slice(yy):
        wait_recv(x.at[yy * 2 + 1 - core], in_sib_recv.at[yy])

    forward(j, range(depth), 0)
    for load in loads:
        load.wait()
    for n, which in enumerate((expert, py * 2 + 1 - core)):
        chosen = jnp.where(ids_v[...] == which, ints_v[...].astype(F32) / 65536.0, 0.0)
        row = jnp.sum(chosen, axis=0, keepdims=True)
        column = jnp.broadcast_to(row, (8, total)).T[:, :1]
        for sec in range(2 * depth):
            weight[n, spot(sec // 2, sec % 2)] = column[sec * rows : (sec + 1) * rows]
    project(py * 2 + core, True)
    forward(1 - j, range(half), lax.div(z, half) * half)
    sib_slice(py)
    project(py * 2 + 1 - core, False)
    forward(1 - j, range(half, depth), half - lax.div(z, half) * half)
    project((1 - py) * 2 + core, False)
    sib_slice(1 - py)
    project((1 - py) * 2 + 1 - core, False)

    def activate(span):
        mean_sq = jnp.sum(ss[span], axis=-1, keepdims=True) / features
        both = acc[span] * lax.rsqrt(mean_sq + EPS)
        gate, up = both[:, :hid], both[:, hid:]
        inner[0, span] = (gate / (1.0 + jnp.exp(-gate)) * up).astype(BF16)

    tiles(activate)

    inner_copy = pltpu.make_async_remote_copy(
        src_ref=inner.at[0], dst_ref=inner.at[1], send_sem=inner_send, recv_sem=inner_recv,
        device_id=sib_dev, device_id_type=MESH,
    )
    inner_copy.start()

    def down(yy, n):
        def one(span):
            product = (
                jnp.dot(inner[n, span], w_out[n, yy], preferred_element_type=F32) * weight[n, span]
            )
            own[yy, span] = own[yy, span] + product if n else product
        tiles(one)

    for load in out_loads:
        load.wait()
    for yy in (1 - py, py):
        down(yy, 0)
    for copy in w_copies:
        copy.wait_recv()
    inner_copy.wait_recv()

    def mine(zz, ii, jj, p):
        xx, yy = place(zz, ii, jj)
        return own[yy, spot(zz, xx), columns(p)]

    def send(value, source, target, slot, p, send_sem, recv_sem, dev):
        source[slot, :, columns(p)] = value.astype(BF16)
        pltpu.make_async_remote_copy(
            src_ref=source.at[slot, :, columns(p)], dst_ref=target.at[slot, :, columns(p)],
            send_sem=send_sem, recv_sem=recv_sem, device_id=dev, device_id_type=MESH,
        ).start()

    def take(target, slot, p, recv_sem):
        wait_recv(target.at[slot, :, columns(p)], recv_sem.at[slot * PARTS + p])
        return target[slot, :, columns(p)].astype(F32)

    order = list(range(half, depth)) + list(range(1, half)) + [0]
    for yy, jj in ((1 - py, 1 - j), (py, j)):
        down(yy, 1)
        for k in order:
            zz = flip(z, k)
            slot = jj * depth + zz
            for p in range(PARTS):
                send(
                    mine(zz, 1 - i, jj, p), b_s, b_r, slot, p,
                    b_send, b_recv.at[slot * PARTS + p], b_dev,
                )
    wait_send(x.at[0, pl.ds(0, (depth - 1) * rows)], in_z_send)
    wait_send(x.at[0, pl.ds(0, depth * rows)], in_a_send)
    wait_send(x.at[0], in_b_send)
    wait_send(x.at[pl.ds(0, 2)], in_sib_send)
    for copy in w_copies + [inner_copy]:
        copy.wait_send()
    for k in order:
        zz = flip(z, k)
        for p in range(PARTS):
            value = mine(zz, i, 1 - j, p) + take(b_r, (1 - j) * depth + zz, p, b_recv)
            send(value, a_s, a_r, zz, p, a_send, a_recv.at[zz * PARTS + p], a_dev)
    last = []
    for k in order:
        zz = flip(z, k)
        for p in range(PARTS):
            value = (
                mine(zz, i, j, p)
                + take(b_r, j * depth + zz, p, b_recv)
                + take(a_r, zz, p, a_recv)
            )
            if k:
                send(value, z_s, z_r, k - 1, p, z_send, z_recv.at[p], z_devs[k - 1])
            else:
                own_part = x[expert, spot(z, px), columns(p)]
                last.append(value + own_part.astype(F32))
    wait_send(b_s, b_send)
    wait_send(a_s, a_send)
    for p in range(PARTS):
        wait_recv(z_r.at[:, :, columns(p)], z_recv.at[p])
        value = last[p]
        for k in range(1, depth):
            value = value + z_r[k - 1, :, columns(p)].astype(F32)
        out[:, columns(p)] = value.astype(BF16)
    wait_send(z_s, z_send)


def body(tokens, gains, w_gate, w_up, w_down, expert_ids, gate_ints, *, sections, experts):
    rows, width = tokens.shape
    hid = w_gate.shape[2]
    features = gains.shape[0]
    total = expert_ids.shape[0]
    top = expert_ids.shape[1]
    depth = sections // 2
    dma = pltpu.SemaphoreType.DMA
    blocks = 4 * depth
    return pl.pallas_call(
        functools.partial(kernel, depth),
        out_shape=jax.ShapeDtypeStruct((rows, width), BF16),
        in_specs=[pl.BlockSpec(memory_space=pl.ANY)] * 7,
        out_specs=pl.BlockSpec(memory_space=pltpu.VMEM),
        scratch_shapes=[
            pltpu.VMEM((experts, total, width), BF16),
            pltpu.VMEM((TILE, width), BF16),
            pltpu.VMEM((features, 2 * hid), BF16),
            pltpu.VMEM((2, 2, hid, width), BF16),
            pltpu.VMEM((experts, 1, width), F32),
            pltpu.VMEM((top, total), jnp.int32),
            pltpu.VMEM((top, total), jnp.int32),
            pltpu.VMEM((2, total, hid), BF16),
            pltpu.VMEM((2, total, 1), F32),
            pltpu.VMEM((total, LANES), F32),
            pltpu.VMEM((total, 2 * hid), F32),
            pltpu.VMEM((2, total, width), F32),
            pltpu.VMEM((2 * depth, rows, width), BF16),
            pltpu.VMEM((2 * depth, rows, width), BF16),
            pltpu.VMEM((depth, rows, width), BF16),
            pltpu.VMEM((depth, rows, width), BF16),
            pltpu.VMEM((depth - 1, rows, width), BF16),
            pltpu.VMEM((depth - 1, rows, width), BF16),
            dma((6 + 2 * experts,)),
            dma((PARTS * blocks,)), dma((2,)), dma, dma, dma, dma,
            dma((2,)), dma((2,)), dma, dma,
            dma, dma((PARTS * 2 * depth,)),
            dma, dma((PARTS * depth,)),
            dma, dma((PARTS,)),
        ],
        compiler_params=pltpu.CompilerParams(
            collective_id=0, has_side_effects=True, vmem_limit_bytes=62 * 1024 * 1024,
        ),
    )(tokens, gains.reshape(experts, 1, width), w_gate, w_up, w_down, expert_ids.T, gate_ints.T)


def solution(mesh):
    in_specs = (
        P("section", "expert"),
        P(),
        P("expert", None, "section"),
        P("expert", None, "section"),
        P("expert", "section", None),
        P(),
        P(),
    )
    run = functools.partial(
        body, sections=mesh.shape["section"], experts=mesh.shape["expert"]
    )
    return jax.shard_map(
        run, mesh=mesh, in_specs=in_specs, out_specs=P("section", "expert"), check_vma=False
    )
```

```python
import functools

import jax
import jax.numpy as jnp
from jax import lax
from jax.experimental import pallas as pl
from jax.experimental.pallas import tpu as pltpu
from jax.sharding import PartitionSpec as P

EPS = 1e-05
MESH = pl.DeviceIdType.MESH
BF16 = jnp.bfloat16
F32 = jnp.float32
TILE = 128
LANES = 128
PARTS = 2


def flip(index, mask):
    bit = 1
    while bit <= mask:
        if mask & bit:
            index = index + bit - 2 * bit * lax.rem(lax.div(index, bit), 2)
        bit *= 2
    return index


def kernel(
    depth, tok, gains, wg, wu, wd, ids, ints, out,
    x, xn, w_in, w_out, gains_v, ids_v, ints_v, inner, weight, ss, acc,
    own, b_s, b_r, a_s, a_r, z_s, z_r,
    load_sem, in_recv, in_sib_recv, in_z_send, in_a_send, in_b_send, in_sib_send,
    w_send, w_recv, inner_send, inner_recv, b_send, b_recv, a_send, a_recv, z_send, z_recv,
):
    section, expert = lax.axis_index("section"), lax.axis_index("expert")
    z, px = lax.div(section, 2), lax.rem(section, 2)
    py, core = lax.div(expert, 2), lax.rem(expert, 2)
    rows, width = tok.shape
    total = x.shape[1]
    hid = wg.shape[2]
    features = x.shape[0] * width
    i = py * (1 - core) + px * core
    j = px * (1 - core) + py * core

    def place(zz, ii, jj):
        yy = ii * (1 - core) + jj * core
        xx = jj * (1 - core) + ii * core
        return xx, yy

    def spot(zz, xx, count=1):
        return pl.ds(pl.multiple_of((xx * depth + zz) * rows, rows), count * rows)

    def device(zz, ii, jj):
        xx, yy = place(zz, ii, jj)
        return zz * 2 + xx, yy * 2 + core

    a_dev = device(z, i, 1 - j)
    b_dev = device(z, 1 - i, j)
    sib_dev = (section, py * 2 + 1 - core)
    z_devs = [(flip(z, k) * 2 + px, expert) for k in range(1, depth)]

    own_block = x.at[expert, spot(z, px)]
    tok_load = pltpu.make_async_copy(tok, own_block, load_sem.at[0])
    tok_load.start()
    loads = [
        pltpu.make_async_copy(gains, gains_v, load_sem.at[1]),
        pltpu.make_async_copy(ids, ids_v, load_sem.at[2]),
        pltpu.make_async_copy(ints, ints_v, load_sem.at[3]),
    ]
    for e in range(x.shape[0]):
        part = pl.ds(e * width, width)
        for n, w in enumerate((wg, wu)):
            loads.append(
                pltpu.make_async_copy(
                    w.at[0, part], w_in.at[part, pl.ds(n * hid, hid)], load_sem.at[4 + 2 * e + n]
                )
            )

    def wd_slice(e):
        return wd.at[0, :, pl.ds(pl.multiple_of(e * width, width), width)]

    out_loads = [
        pltpu.make_async_copy(
            wd_slice(yy * 2 + core), w_out.at[0, yy], load_sem.at[4 + 2 * x.shape[0] + yy]
        )
        for yy in range(2)
    ]
    barrier = pltpu.get_barrier_semaphore()
    partners = z_devs + [a_dev, b_dev, sib_dev]
    for partner in partners:
        pl.semaphore_signal(barrier, inc=1, device_id=partner, device_id_type=MESH)
    for load in loads + out_loads:
        load.start()
    pl.semaphore_wait(barrier, len(partners))
    tok_load.wait()

    half = depth // 2

    def columns(p):
        return pl.ds(p * (width // PARTS), width // PARTS)

    def block(zz, ii, jj, p):
        xx, yy = place(zz, ii, jj)
        return x.at[yy * 2 + core, spot(zz, xx), columns(p)]

    def mark(zz, ii, jj, p):
        return in_recv.at[((zz * 2 + ii) * 2 + jj) * PARTS + p]

    def push(zz, ii, jj, p, send_sem, target):
        here = block(zz, ii, jj, p)
        pltpu.make_async_remote_copy(
            src_ref=here, dst_ref=here, send_sem=send_sem, recv_sem=mark(zz, ii, jj, p),
            device_id=target, device_id_type=MESH,
        ).start()

    def push_sib(ii, jj, first, count):
        xx, yy = place(z, ii, jj)
        here = x.at[yy * 2 + core, spot(first, xx, count)]
        pltpu.make_async_remote_copy(
            src_ref=here, dst_ref=here, send_sem=in_sib_send, recv_sem=in_sib_recv.at[yy],
            device_id=sib_dev, device_id_type=MESH,
        ).start()

    def wait_recv(ref, sem):
        pltpu.make_async_remote_copy(
            src_ref=ref, dst_ref=ref, send_sem=in_z_send, recv_sem=sem,
            device_id=sib_dev, device_id_type=MESH,
        ).wait_recv()

    def wait_send(ref, sem):
        pltpu.make_async_remote_copy(
            src_ref=ref, dst_ref=ref, send_sem=sem, recv_sem=in_recv.at[0],
            device_id=sib_dev, device_id_type=MESH,
        ).wait_send()

    def arrived(zz, ii, jj, p):
        wait_recv(block(zz, ii, jj, p), mark(zz, ii, jj, p))

    for p in range(PARTS):
        for k in [half] + list(range(1, half)):
            push(z, i, j, p, in_z_send, z_devs[k - 1])
        push(z, i, j, p, in_a_send, a_dev)
        push(z, i, j, p, in_b_send, b_dev)
    w_copies = [
        pltpu.make_async_remote_copy(
            src_ref=wd_slice(yy * 2 + 1 - core), dst_ref=w_out.at[1, yy],
            send_sem=w_send.at[yy], recv_sem=w_recv.at[yy],
            device_id=sib_dev, device_id_type=MESH,
        )
        for yy in range(2)
    ]
    for k in [half] + list(range(1, half)) + list(range(half + 1, depth)):
        zz = flip(z, k)
        for p in range(PARTS):
            arrived(zz, i, j, p)
            if k == half:
                for n in range(1, half):
                    push(zz, i, j, p, in_z_send, z_devs[n - 1])
            push(zz, i, j, p, in_a_send, a_dev)
            push(zz, i, j, p, in_b_send, b_dev)
    push_sib(i, j, 0, depth)
    for copy in w_copies:
        copy.start()
    for k in range(depth):
        zz = flip(z, k)
        for p in range(PARTS):
            arrived(zz, i, 1 - j, p)
            push(zz, i, 1 - j, p, in_b_send, b_dev)
    push_sib(i, 1 - j, 0, depth)

    def tiles(body):
        if total == TILE:
            body(pl.ds(0, TILE))
        else:
            @pl.loop(0, total // TILE)
            def _(t):
                body(pl.ds(pl.multiple_of(t * TILE, TILE), TILE))

    def project(e, first):
        def one(span):
            squares = jnp.zeros((TILE, LANES), F32) if first else ss[span]
            for c in range(0, width, LANES):
                cols = pl.ds(c, LANES)
                part = x[e, span, cols].astype(F32)
                squares = squares + part * part
                xn[:, cols] = (part * gains_v[e, :, cols]).astype(BF16)
            ss[span] = squares
            product = jnp.dot(
                xn[...], w_in[pl.ds(pl.multiple_of(e * width, width), width)],
                preferred_element_type=F32,
            )
            acc[span] = product if first else acc[span] + product
        tiles(one)

    def forward(jj, ks, first):
        for k in ks:
            for p in range(PARTS):
                arrived(flip(z, k), 1 - i, jj, p)
        push_sib(1 - i, jj, first, len(ks))

    def sib_slice(yy):
        wait_recv(x.at[yy * 2 + 1 - core], in_sib_recv.at[yy])

    forward(j, range(depth), 0)
    for load in loads:
        load.wait()
    for n, which in enumerate((expert, py * 2 + 1 - core)):
        chosen = jnp.where(ids_v[...] == which, ints_v[...].astype(F32) / 65536.0, 0.0)
        row = jnp.sum(chosen, axis=0, keepdims=True)
        column = jnp.broadcast_to(row, (8, total)).T[:, :1]
        for sec in range(2 * depth):
            weight[n, spot(sec // 2, sec % 2)] = column[sec * rows : (sec + 1) * rows]
    project(py * 2 + core, True)
    forward(1 - j, range(half), lax.div(z, half) * half)
    sib_slice(py)
    project(py * 2 + 1 - core, False)
    forward(1 - j, range(half, depth), half - lax.div(z, half) * half)
    project((1 - py) * 2 + core, False)
    sib_slice(1 - py)
    project((1 - py) * 2 + 1 - core, False)

    def activate(span):
        mean_sq = jnp.sum(ss[span], axis=-1, keepdims=True) / features
        both = acc[span] * lax.rsqrt(mean_sq + EPS)
        gate, up = both[:, :hid], both[:, hid:]
        inner[0, span] = (gate / (1.0 + jnp.exp(-gate)) * up).astype(BF16)

    tiles(activate)

    inner_copy = pltpu.make_async_remote_copy(
        src_ref=inner.at[0], dst_ref=inner.at[1], send_sem=inner_send, recv_sem=inner_recv,
        device_id=sib_dev, device_id_type=MESH,
    )
    inner_copy.start()

    def down(yy, n):
        def one(span):
            product = (
                jnp.dot(inner[n, span], w_out[n, yy], preferred_element_type=F32) * weight[n, span]
            )
            own[yy, span] = own[yy, span] + product if n else product
        tiles(one)

    for load in out_loads:
        load.wait()
    for yy in (1 - py, py):
        down(yy, 0)
    for copy in w_copies:
        copy.wait_recv()
    inner_copy.wait_recv()

    def mine(zz, ii, jj, p):
        xx, yy = place(zz, ii, jj)
        return own[yy, spot(zz, xx), columns(p)]

    def send(value, source, target, slot, p, send_sem, recv_sem, dev):
        source[slot, :, columns(p)] = value.astype(BF16)
        pltpu.make_async_remote_copy(
            src_ref=source.at[slot, :, columns(p)], dst_ref=target.at[slot, :, columns(p)],
            send_sem=send_sem, recv_sem=recv_sem, device_id=dev, device_id_type=MESH,
        ).start()

    def take(target, slot, p, recv_sem):
        wait_recv(target.at[slot, :, columns(p)], recv_sem.at[slot * PARTS + p])
        return target[slot, :, columns(p)].astype(F32)

    order = list(range(half + 1, depth)) + list(range(1, half)) + [half, 0]
    for yy, jj in ((1 - py, 1 - j), (py, j)):
        down(yy, 1)
        for k in order:
            zz = flip(z, k)
            slot = jj * depth + zz
            for p in range(PARTS):
                send(
                    mine(zz, 1 - i, jj, p), b_s, b_r, slot, p,
                    b_send, b_recv.at[slot * PARTS + p], b_dev,
                )
    wait_send(x.at[0, pl.ds(0, (depth - 1) * rows)], in_z_send)
    wait_send(x.at[0, pl.ds(0, depth * rows)], in_a_send)
    wait_send(x.at[0], in_b_send)
    wait_send(x.at[pl.ds(0, 2)], in_sib_send)
    for copy in w_copies + [inner_copy]:
        copy.wait_send()
    for k in order:
        zz = flip(z, k)
        for p in range(PARTS):
            value = mine(zz, i, 1 - j, p) + take(b_r, (1 - j) * depth + zz, p, b_recv)
            send(value, a_s, a_r, zz, p, a_send, a_recv.at[zz * PARTS + p], a_dev)
    last = []
    for k in order:
        zz = flip(z, k)
        for p in range(PARTS):
            value = (
                mine(zz, i, j, p)
                + take(b_r, j * depth + zz, p, b_recv)
                + take(a_r, zz, p, a_recv)
            )
            if k == half and half > 1:
                wait_recv(z_r.at[pl.ds(half, half - 1), :, columns(p)], z_recv.at[PARTS + p])
                for n in range(half, depth - 1):
                    value = value + z_r[n, :, columns(p)].astype(F32)
            if k:
                relay = k > half
                send(
                    value, z_s, z_r, k - 1, p, z_send, z_recv.at[PARTS * relay + p],
                    z_devs[k - half - 1 if relay else k - 1],
                )
            else:
                own_part = x[expert, spot(z, px), columns(p)]
                last.append(value + own_part.astype(F32))
    wait_send(b_s, b_send)
    wait_send(a_s, a_send)
    for p in range(PARTS):
        wait_recv(z_r.at[pl.ds(0, half), :, columns(p)], z_recv.at[p])
        value = last[p]
        for k in range(1, half + 1):
            value = value + z_r[k - 1, :, columns(p)].astype(F32)
        out[:, columns(p)] = value.astype(BF16)
    wait_send(z_s, z_send)


def body(tokens, gains, w_gate, w_up, w_down, expert_ids, gate_ints, *, sections, experts):
    rows, width = tokens.shape
    hid = w_gate.shape[2]
    features = gains.shape[0]
    total = expert_ids.shape[0]
    top = expert_ids.shape[1]
    depth = sections // 2
    dma = pltpu.SemaphoreType.DMA
    blocks = 4 * depth
    return pl.pallas_call(
        functools.partial(kernel, depth),
        out_shape=jax.ShapeDtypeStruct((rows, width), BF16),
        in_specs=[pl.BlockSpec(memory_space=pl.ANY)] * 7,
        out_specs=pl.BlockSpec(memory_space=pltpu.VMEM),
        scratch_shapes=[
            pltpu.VMEM((experts, total, width), BF16),
            pltpu.VMEM((TILE, width), BF16),
            pltpu.VMEM((features, 2 * hid), BF16),
            pltpu.VMEM((2, 2, hid, width), BF16),
            pltpu.VMEM((experts, 1, width), F32),
            pltpu.VMEM((top, total), jnp.int32),
            pltpu.VMEM((top, total), jnp.int32),
            pltpu.VMEM((2, total, hid), BF16),
            pltpu.VMEM((2, total, 1), F32),
            pltpu.VMEM((total, LANES), F32),
            pltpu.VMEM((total, 2 * hid), F32),
            pltpu.VMEM((2, total, width), F32),
            pltpu.VMEM((2 * depth, rows, width), BF16),
            pltpu.VMEM((2 * depth, rows, width), BF16),
            pltpu.VMEM((depth, rows, width), BF16),
            pltpu.VMEM((depth, rows, width), BF16),
            pltpu.VMEM((depth - 1, rows, width), BF16),
            pltpu.VMEM((depth - 1, rows, width), BF16),
            dma((6 + 2 * experts,)),
            dma((PARTS * blocks,)), dma((2,)), dma, dma, dma, dma,
            dma((2,)), dma((2,)), dma, dma,
            dma, dma((PARTS * 2 * depth,)),
            dma, dma((PARTS * depth,)),
            dma, dma((2 * PARTS,)),
        ],
        compiler_params=pltpu.CompilerParams(
            collective_id=0, has_side_effects=True, vmem_limit_bytes=62 * 1024 * 1024,
        ),
    )(tokens, gains.reshape(experts, 1, width), w_gate, w_up, w_down, expert_ids.T, gate_ints.T)


def solution(mesh):
    in_specs = (
        P("section", "expert"),
        P(),
        P("expert", None, "section"),
        P("expert", None, "section"),
        P("expert", "section", None),
        P(),
        P(),
    )
    run = functools.partial(
        body, sections=mesh.shape["section"], experts=mesh.shape["expert"]
    )
    return jax.shard_map(
        run, mesh=mesh, in_specs=in_specs, out_specs=P("section", "expert"), check_vma=False
    )
```
